32 devices in a mesh: row: 8 (over z, x), col: 4 (over y, core).
Axes of the slice: x: 2, y: 2, z: 4, core: 2. Of those that a mesh axis runs over, the one named last changes fastest.
Arguments:
- features: bfloat16 [48, 512, 512], P(None, 'row', 'col'), may hold values from -6 to 6
- w_dilated: bfloat16 [2, 3, 3, 48, 48], replicated, may hold values from -0.3125 to 0.3125
- w_pointwise: bfloat16 [2, 48, 48], replicated, may hold values from -0.875 to 0.875
- norm_gain: float32 [2, 2, 48], replicated, may hold values from 0.25 to 1.75
- norm_bias: float32 [2, 2, 48], replicated, may hold values from -0.5 to 0.5
Outputs:
- refined: bfloat16 [48, 512, 512], P(None, 'row', 'col')
The draws below stay inside these ranges and needn't reach their ends.
All inputs are finite; a program needn't handle non-finite values.
Results may differ from the reference program's by a relative error of at most 0.0065.
Values may be sent and summed in bfloat16 or wider, within the bound.
A program may use at most 64 MiB of HBM per device.

```python
import jax
import jax.numpy as jnp
from jax import lax

CH = 48
FIRST_DILATION = 8
SECOND_DILATION = 16
TR = 64
N = 512


def level_of(rng, dims, pieces, least, largest):
    def one(axis_at, shards_of):
        heights = jax.random.uniform(jax.random.fold_in(jax.random.fold_in(rng, 6), axis_at), (shards_of,), jnp.float32, least / len(pieces), largest / len(pieces))
        return jnp.repeat(jnp.exp(heights), dims[axis_at] // shards_of).reshape((-1,) + (1,) * (len(dims) - axis_at - 1))

    gain = one(*pieces[0])
    for cut in pieces[1:]:
        gain = gain * one(*cut)
    return gain


def gaussian(rng, extent, width, reach, pieces=(), held_as=jnp.bfloat16):
    level = level_of(rng, extent, pieces, -0.22, 0.18) if pieces else 1.0
    values = jax.random.normal(rng, extent, jnp.float32) * width * level
    return jnp.minimum(jnp.maximum(values, -reach), reach).astype(held_as)


def setup_inputs(seed: int = 0) -> dict:
    streams_of = jax.random.split(jax.random.key(seed), 6)
    return {
        "features": gaussian(streams_of[0], (CH, N, N), 1.0, 6.0, ((1, 8), (2, 4))),
        "w_dilated": gaussian(streams_of[1], (2, 3, 3, CH, CH), (9 * CH) ** -0.5, 0.3125),
        "w_pointwise": gaussian(streams_of[2], (2, CH, CH), CH ** -0.5, 0.875),
        "norm_gain": jnp.clip(1.0 + 0.15 * jax.random.normal(streams_of[3], (2, 2, CH), jnp.float32), 0.25, 1.75),
        "norm_bias": jnp.clip(jax.random.uniform(streams_of[4], (2, 2, CH), jnp.float32, -0.5, 0.5), -0.5, 0.5),
    }


def dilated_terms(segment, kernel, gain_pair, bias_pair, pointwise, dilation_rate):
    active = jnp.maximum(segment.astype(jnp.float32), 0.0)
    spread = lax.conv_general_dilated(active[None], kernel.astype(jnp.float32), (1, 1), "VALID", rhs_dilation=(dilation_rate, dilation_rate), precision=lax.Precision.HIGHEST)[0]
    hidden = jnp.maximum(spread * gain_pair[0][:, None, None] + bias_pair[0][:, None, None], 0.0).astype(jnp.bfloat16)
    branch = jnp.einsum("oc,chw->ohw", pointwise.astype(jnp.float32), hidden.astype(jnp.float32), precision=lax.Precision.HIGHEST)
    return branch * gain_pair[1][:, None, None] + bias_pair[1][:, None, None]


def residual_block(current_state, kernel, gain_pair, bias_pair, pointwise, dilation_rate):
    height = TR
    strips = N // height
    anchor = jnp.zeros((), jnp.int32)
    padded = jnp.pad(current_state, ((0, 0), (dilation_rate, dilation_rate), (dilation_rate, dilation_rate)))

    def strip_block(position_index):
        offset = (position_index * height).astype(jnp.int32)
        segment = lax.dynamic_slice(padded, (anchor, offset, anchor), (CH, height + 2 * dilation_rate, N + 2 * dilation_rate))
        own_rows = lax.dynamic_slice(current_state, (anchor, offset, anchor), (CH, height, N))
        terms = dilated_terms(segment, kernel, gain_pair, bias_pair, pointwise, dilation_rate)
        return (own_rows.astype(jnp.float32) + terms).astype(jnp.bfloat16)

    stacked = lax.map(strip_block, jnp.arange(strips, dtype=jnp.int32))
    output_map = jnp.transpose(stacked, (1, 0, 2, 3)).reshape(CH, N, N)
    output_map = lax.optimization_barrier(output_map)

    def symmetrize(position_index):
        offset = (position_index * height).astype(jnp.int32)
        row_part = lax.dynamic_slice(output_map, (anchor, offset, anchor), (CH, height, N)).astype(jnp.float32)
        col_part = lax.dynamic_slice(output_map, (anchor, anchor, offset), (CH, N, height)).astype(jnp.float32)
        return ((row_part + jnp.swapaxes(col_part, 1, 2)) * 0.5).astype(jnp.bfloat16)

    halves = lax.map(symmetrize, jnp.arange(strips, dtype=jnp.int32))
    return jnp.transpose(halves, (1, 0, 2, 3)).reshape(CH, N, N)


def reference(features, w_dilated, w_pointwise, norm_gain, norm_bias):
    current_state = features
    for layer_index in range(2):
        dilation_rate = FIRST_DILATION if layer_index == 0 else SECOND_DILATION
        kernel = jnp.transpose(w_dilated[layer_index], (2, 3, 0, 1))
        current_state = residual_block(current_state, kernel, norm_gain[layer_index], norm_bias[layer_index], w_pointwise[layer_index], dilation_rate)
    return current_state
```

```python
import functools

import jax
import jax.numpy as jnp
from jax import lax
from jax.experimental import pallas as pl
from jax.experimental.pallas import tpu as pltpu
from jax.sharding import PartitionSpec as P

FIRST_DILATION = 8
SECOND_DILATION = 16
SIDE = 16
PACK = 8
MESH = pl.DeviceIdType.MESH
BF16 = jnp.bfloat16
F32 = jnp.float32

DIRECTIONS = ((1, 0), (-1, 0), (0, 1), (0, -1), (1, 1), (-1, 1), (1, -1), (-1, -1))


def inside(r, c, n_row, n_col):
    return (r >= 0) & (r < n_row) & (c >= 0) & (c < n_col)


def pack_sides(main, offset, side_first, side_last, groups, tc):
    @pl.loop(0, groups)
    def _(g):
        rows = [main[offset + g * PACK + k] for k in range(PACK)]
        side_first[g] = jnp.concatenate([x[:, :SIDE] for x in rows], axis=1)
        side_last[g] = jnp.concatenate([x[:, tc - SIDE :] for x in rows], axis=1)


def halo(main, left, right, side_first, side_last, d, tr, n_row, n_col, send, recv):
    r, c = lax.axis_index("row"), lax.axis_index("col")
    hg, groups = d // PACK, tr // PACK
    moves = []
    for n, (dr, dc) in enumerate(DIRECTIONS):
        if dc == 0:
            src = main.at[pl.ds(tr, d)] if dr == 1 else main.at[pl.ds(d, d)]
            dst = main.at[pl.ds(0, d)] if dr == 1 else main.at[pl.ds(tr + d, d)]
        else:
            from_ref = side_last if dc == 1 else side_first
            to_ref = left if dc == 1 else right
            if dr == 0:
                src, dst = from_ref, to_ref.at[pl.ds(hg, groups)]
            elif dr == 1:
                src, dst = from_ref.at[pl.ds(groups - hg, hg)], to_ref.at[pl.ds(0, hg)]
            else:
                src, dst = from_ref.at[pl.ds(0, hg)], to_ref.at[pl.ds(groups + hg, hg)]
        copy = pltpu.make_async_remote_copy(
            src_ref=src,
            dst_ref=dst,
            send_sem=send.at[n],
            recv_sem=recv.at[n],
            device_id=(r + dr, c + dc),
            device_id_type=MESH,
        )
        sends = inside(r + dr, c + dc, n_row, n_col)
        receives = inside(r - dr, c - dc, n_row, n_col)
        moves.append((copy, sends, receives, dst))
    return moves


def start(moves):
    for copy, sends, _, _ in moves:
        pl.when(sends)(copy.start)


def clear(moves):
    for _, _, receives, dst in moves:

        @pl.when(jnp.logical_not(receives))
        def _():
            dst[...] = jnp.zeros(dst.shape, dst.dtype)


def finish(moves):
    for copy, _, receives, _ in moves:
        pl.when(receives)(copy.wait_recv)


def finish_sends(moves):
    for copy, sends, _, _ in moves:
        pl.when(sends)(copy.wait_send)


def taps(main, left, right, weights, spread, d, tr, tc):
    height = weights.shape[0]

    @pl.loop(0, (tr + 2 * d) // PACK)
    def _(g):
        lg, rg = left[g], right[g]
        for k in range(0, PACK, 2):
            columns = []
            for u in (k, k + 1):
                x = main[g * PACK + u]
                before = jnp.concatenate(
                    [lg[:, SIDE * u + SIDE - d : SIDE * u + SIDE], x[:, : tc - d]], axis=1
                )
                after = jnp.concatenate([x[:, d:], rg[:, SIDE * u : SIDE * u + d]], axis=1)
                columns.append(jnp.concatenate([before, x, after], axis=0))
            active = jnp.maximum(jnp.concatenate(columns, axis=1), jnp.zeros((), BF16))
            out = jnp.dot(weights[...], active, preferred_element_type=F32)
            spread[g * PACK + k, :height] = out[:, :tc]
            spread[g * PACK + k + 1, :height] = out[:, tc:]


def block_rows(spread, base, row, d, ch, scale, layer):
    total = (
        spread[row, base : base + ch]
        + spread[row + d, base + ch : base + 2 * ch]
        + spread[row + 2 * d, base + 2 * ch : base + 3 * ch]
    )
    return jnp.maximum(total * scale[4 * layer] + scale[4 * layer + 2], 0.0).astype(BF16)


def kernel(
    n_row, n_col, tile, turned, w_first, w_turned, w_second, w_point, scale, out,
    fx, tx, sx, fl, fr, tl, tr_, sl, sr, ff, flast, tf, tlast, sf, slast,
    y0, mirror, spread, local, m_send, m_recv, h_send, h_recv,
):
    r, c = lax.axis_index("row"), lax.axis_index("col")
    rows, ch, tc = tile.shape
    ratio = tc // rows
    d0, d1 = FIRST_DILATION, SECOND_DILATION

    own = pltpu.make_async_copy(tile, fx.at[pl.ds(d0, rows)], local.at[0])
    own.start()

    partners = [(ratio * c + h, r // ratio) for h in range(ratio)]
    others = [(pr != r) | (pc != c) for pr, pc in partners]

    barrier = pltpu.get_barrier_semaphore()
    expected = jnp.int32(0)
    for dr, dc in DIRECTIONS:
        there = inside(r + dr, c + dc, n_row, n_col)
        expected = expected + there.astype(jnp.int32)

        @pl.when(there)
        def _():
            pl.semaphore_signal(
                barrier, inc=1, device_id=(r + dr, c + dc), device_id_type=MESH
            )

    for partner, other in zip(partners, others):
        expected = expected + other.astype(jnp.int32)

        @pl.when(other)
        def _():
            pl.semaphore_signal(barrier, inc=1, device_id=partner, device_id_type=MESH)

    pl.semaphore_wait(barrier, expected)

    mine = lax.rem(r, ratio)
    swaps = []
    for h in range(ratio):
        copy = pltpu.make_async_remote_copy(
            src_ref=turned.at[h],
            dst_ref=mirror.at[mine],
            send_sem=m_send.at[h],
            recv_sem=m_recv.at[mine],
            device_id=partners[h],
            device_id_type=MESH,
        )
        arrival = pltpu.make_async_remote_copy(
            src_ref=turned.at[h],
            dst_ref=mirror.at[h],
            send_sem=m_send.at[h],
            recv_sem=m_recv.at[h],
            device_id=partners[h],
            device_id_type=MESH,
        )
        stay = pltpu.make_async_copy(turned.at[h], mirror.at[h], local.at[1])
        pl.when(others[h])(copy.start)
        pl.when(jnp.logical_not(others[h]))(stay.start)
        swaps.append((copy, arrival, stay, others[h]))

    own.wait()
    groups = rows // PACK
    f_halo = halo(fx, fl, fr, ff, flast, d0, rows, n_row, n_col, h_send.at[0], h_recv.at[0])
    start(f_halo[:2])
    pack_sides(fx, d0, ff, flast, groups, tc)
    start(f_halo[2:])
    t_halo = halo(tx, tl, tr_, tf, tlast, d0, rows, n_row, n_col, h_send.at[1], h_recv.at[1])
    s_halo = halo(sx, sl, sr, sf, slast, d1, rows, n_row, n_col, h_send.at[2], h_recv.at[2])
    clear(f_halo)
    clear(t_halo)
    clear(s_halo)
    finish(f_halo)

    taps(fx, fl, fr, w_first, spread, d0, rows, tc)
    unroll = 4

    @pl.loop(0, rows // unroll)
    def _(t):
        hidden = [
            block_rows(spread, 0, t * unroll + u, d0, ch, scale, 0) for u in range(unroll)
        ]
        branch = jnp.dot(
            w_point[0], jnp.concatenate(hidden, axis=1), preferred_element_type=F32
        )
        for u in range(unroll):
            row = t * unroll + u
            y = branch[:, u * tc : (u + 1) * tc] * scale[1] + scale[3]
            y0[row] = (fx[d0 + row].astype(F32) + y).astype(BF16)

    for copy, arrival, stay, other in swaps:
        pl.when(other)(arrival.wait_recv)
        pl.when(jnp.logical_not(other))(stay.wait)

    half = rows // ratio

    @pl.loop(0, half)
    def _(j):
        pieces = [mirror[h, j] for h in range(ratio)]
        for k in range(ratio):
            tx[d0 + k * half + j] = jnp.concatenate(
                [x[:, k * rows : (k + 1) * rows] for x in pieces], axis=1
            )

    start(t_halo[:2])
    pack_sides(tx, d0, tf, tlast, groups, tc)
    start(t_halo[2:])
    finish(t_halo)
    taps(tx, tl, tr_, w_turned, spread, d0, rows, tc)

    @pl.loop(0, rows // unroll)
    def _(t):
        hidden = [
            block_rows(spread, 0, t * unroll + u, d0, ch, scale, 0) for u in range(unroll)
        ]
        branch = jnp.dot(
            w_point[0], jnp.concatenate(hidden, axis=1), preferred_element_type=F32
        )
        for u in range(unroll):
            row = t * unroll + u
            y = branch[:, u * tc : (u + 1) * tc] * scale[1] + scale[3]
            y = (tx[d0 + row].astype(F32) + y).astype(BF16).astype(F32)
            sx[d1 + row] = ((y + y0[row].astype(F32)) * 0.5).astype(BF16)

    start(s_halo[:2])
    pack_sides(sx, d1, sf, slast, groups, tc)
    start(s_halo[2:])
    finish(s_halo)
    taps(sx, sl, sr, w_second, spread, d1, rows, tc)

    @pl.loop(0, rows // 2)
    def _(t):
        hidden = [
            block_rows(spread, base, t * 2 + u, d1, ch, scale, 1)
            for u in range(2)
            for base in (0, 3 * ch)
        ]
        branch = jnp.dot(
            w_point[1], jnp.concatenate(hidden, axis=1), preferred_element_type=F32
        )
        for u in range(2):
            row = t * 2 + u
            x = sx[d1 + row].astype(F32)
            both = []
            for v in (2 * u, 2 * u + 1):
                y = branch[:, v * tc : (v + 1) * tc] * scale[5] + scale[7]
                both.append((x + y).astype(BF16).astype(F32))
            out[row] = ((both[0] + both[1]) * 0.5).astype(BF16)

    for copy, arrival, stay, other in swaps:
        pl.when(other)(copy.wait_send)
    finish_sends(f_halo)
    finish_sends(t_halo)
    finish_sends(s_halo)


def body(features, w_dilated, w_pointwise, norm_gain, norm_bias):
    n_row, n_col = lax.axis_size("row"), lax.axis_size("col")
    ch, rows, tc = features.shape
    ratio = tc // rows
    half = rows // ratio
    tile = jnp.transpose(features, (1, 0, 2))
    turned = jnp.transpose(
        features.reshape(ch, rows, ratio, ratio, half), (2, 4, 0, 3, 1)
    ).reshape(ratio, half, ch, tc)
    straight = jnp.transpose(w_dilated, (0, 1, 3, 2, 4)).reshape(2, 3 * ch, 3 * ch)
    swapped = jnp.transpose(w_dilated, (0, 2, 3, 1, 4)).reshape(2, 3 * ch, 3 * ch)
    second = jnp.concatenate([straight[1], swapped[1]], axis=0)
    scale = jnp.concatenate([norm_gain, norm_bias], axis=1).reshape(8, ch, 1)
    scale = jnp.broadcast_to(scale, (8, ch, tc))
    d0, d1 = FIRST_DILATION, SECOND_DILATION
    groups = rows // PACK

    def vmem(*shape, dtype=BF16):
        return pltpu.VMEM(shape, dtype)

    def border(d):
        return vmem(groups + 2 * d // PACK, ch, tc)

    result = pl.pallas_call(
        functools.partial(kernel, n_row, n_col),
        out_shape=jax.ShapeDtypeStruct((rows, ch, tc), BF16),
        in_specs=[pl.BlockSpec(memory_space=pl.ANY)] * 2
        + [pl.BlockSpec(memory_space=pltpu.VMEM)] * 5,
        out_specs=pl.BlockSpec(memory_space=pltpu.VMEM),
        scratch_shapes=[
            vmem(rows + 2 * d0, ch, tc),
            vmem(rows + 2 * d0, ch, tc),
            vmem(rows + 2 * d1, ch, tc),
            border(d0), border(d0), border(d0), border(d0), border(d1), border(d1),
            *[vmem(groups, ch, tc) for _ in range(6)],
            vmem(rows, ch, tc),
            vmem(ratio, half, ch, tc),
            vmem(rows + 2 * d1, 6 * ch, tc, dtype=F32),
            pltpu.SemaphoreType.DMA((2,)),
            pltpu.SemaphoreType.DMA((ratio,)),
            pltpu.SemaphoreType.DMA((ratio,)),
            pltpu.SemaphoreType.DMA((3, 8)),
            pltpu.SemaphoreType.DMA((3, 8)),
        ],
        compiler_params=pltpu.CompilerParams(
            collective_id=0, has_side_effects=True, vmem_limit_bytes=48 * 1024 * 1024
        ),
        cost_estimate=pl.CostEstimate(
            flops=4 * 2 * 9 * ch * ch * rows * tc, bytes_accessed=6 * ch * rows * tc, transcendentals=0
        ),
    )(tile, turned, straight[0], swapped[0], second, w_pointwise, scale)
    return jnp.transpose(result, (1, 0, 2))


def solution(mesh):
    in_specs = (P(None, "row", "col"), P(), P(), P(), P())
    out_specs = P(None, "row", "col")
    return jax.shard_map(body, mesh=mesh, in_specs=in_specs, out_specs=out_specs, check_vma=False)
```

```python
import functools

import jax
import jax.numpy as jnp
from jax import lax
from jax.experimental import pallas as pl
from jax.experimental.pallas import tpu as pltpu
from jax.sharding import PartitionSpec as P

FIRST_DILATION = 8
SECOND_DILATION = 16
SIDE = 16
PACK = 8
MESH = pl.DeviceIdType.MESH
BF16 = jnp.bfloat16
F32 = jnp.float32

DIRECTIONS = ((1, 0), (-1, 0), (0, 1), (0, -1), (1, 1), (-1, 1), (1, -1), (-1, -1))


def inside(r, c, n_row, n_col):
    return (r >= 0) & (r < n_row) & (c >= 0) & (c < n_col)


def pack_sides(main, offset, side_first, side_last, groups, tc):
    @pl.loop(0, groups)
    def _(g):
        rows = [main[offset + g * PACK + k] for k in range(PACK)]
        side_first[g] = jnp.concatenate([x[:, :SIDE] for x in rows], axis=1)
        side_last[g] = jnp.concatenate([x[:, tc - SIDE :] for x in rows], axis=1)


def halo(main, left, right, side_first, side_last, d, tr, n_row, n_col, send, recv):
    r, c = lax.axis_index("row"), lax.axis_index("col")
    hg, groups = d // PACK, tr // PACK
    moves = []
    for n, (dr, dc) in enumerate(DIRECTIONS):
        if dc == 0:
            src = main.at[pl.ds(tr, d)] if dr == 1 else main.at[pl.ds(d, d)]
            dst = main.at[pl.ds(0, d)] if dr == 1 else main.at[pl.ds(tr + d, d)]
        else:
            from_ref = side_last if dc == 1 else side_first
            to_ref = left if dc == 1 else right
            if dr == 0:
                src, dst = from_ref, to_ref.at[pl.ds(hg, groups)]
            elif dr == 1:
                src, dst = from_ref.at[pl.ds(groups - hg, hg)], to_ref.at[pl.ds(0, hg)]
            else:
                src, dst = from_ref.at[pl.ds(0, hg)], to_ref.at[pl.ds(groups + hg, hg)]
        copy = pltpu.make_async_remote_copy(
            src_ref=src,
            dst_ref=dst,
            send_sem=send.at[n],
            recv_sem=recv.at[n],
            device_id=(r + dr, c + dc),
            device_id_type=MESH,
        )
        sends = inside(r + dr, c + dc, n_row, n_col)
        receives = inside(r - dr, c - dc, n_row, n_col)
        moves.append((copy, sends, receives, dst))
    return moves


def start(moves):
    for copy, sends, _, _ in moves:
        pl.when(sends)(copy.start)


def clear(moves):
    for _, _, receives, dst in moves:

        @pl.when(jnp.logical_not(receives))
        def _():
            dst[...] = jnp.zeros(dst.shape, dst.dtype)


def finish(moves):
    for copy, _, receives, _ in moves:
        pl.when(receives)(copy.wait_recv)


def finish_sends(moves):
    for copy, sends, _, _ in moves:
        pl.when(sends)(copy.wait_send)


def taps(main, left, right, weights, spread, d, tr, tc):
    height = weights.shape[0]

    @pl.loop(0, (tr + 2 * d) // PACK)
    def _(g):
        lg, rg = left[g], right[g]
        for k in range(0, PACK, 2):
            columns = []
            for u in (k, k + 1):
                x = main[g * PACK + u]
                before = jnp.concatenate(
                    [lg[:, SIDE * u + SIDE - d : SIDE * u + SIDE], x[:, : tc - d]], axis=1
                )
                after = jnp.concatenate([x[:, d:], rg[:, SIDE * u : SIDE * u + d]], axis=1)
                columns.append(jnp.concatenate([before, x, after], axis=0))
            active = jnp.maximum(jnp.concatenate(columns, axis=1), jnp.zeros((), BF16))
            out = jnp.dot(weights[...], active, preferred_element_type=F32)
            spread[g * PACK + k, :height] = out[:, :tc]
            spread[g * PACK + k + 1, :height] = out[:, tc:]


def block_rows(spread, base, row, d, ch, scale, layer):
    total = (
        spread[row, base : base + ch]
        + spread[row + d, base + ch : base + 2 * ch]
        + spread[row + 2 * d, base + 2 * ch : base + 3 * ch]
    )
    return jnp.maximum(total * scale[4 * layer] + scale[4 * layer + 2], 0.0).astype(BF16)


def fill_weights(w_taps, w_first, w_turned, w_second, ch):
    for p in range(3):
        for q in range(3):
            for layer, ref, base, tap in (
                (0, w_first, 0, 3 * p + q),
                (0, w_turned, 0, 3 * q + p),
                (1, w_second, 0, 3 * p + q),
                (1, w_second, 3 * ch, 3 * q + p),
            ):
                ref[base + p * ch : base + (p + 1) * ch, q * ch : (q + 1) * ch] = w_taps[
                    9 * layer + tap
                ]


class Swap:
    def __init__(
        self, n_row, n_col, ratio, parcel, mirror, relay, local, m_send, m_recv, l_send, l_recv
    ):
        r, c = lax.axis_index("row"), lax.axis_index("col")
        self.me = (r, c)
        self.ratio = ratio
        self.local = local
        self.cut = parcel.shape[1] // 2
        mine = lax.rem(r, ratio)
        big = r // ratio
        odd, base = lax.rem(c, 2), c // 2
        slots = n_col // 2
        same = lambda a, b: (a[0] == b[0]) & (a[1] == b[1])
        part = lambda ref, piece: ref.at[pl.ds(piece * self.cut, self.cut)]

        def remote(src, dst, send, recv, to):
            return pltpu.make_async_remote_copy(
                src_ref=src, dst_ref=dst, send_sem=send, recv_sem=recv,
                device_id=to, device_id_type=MESH,
            )

        self.out = []
        for piece in (0, 1):
            for h in range(ratio):
                goal = (ratio * c + h, big)
                if piece == 0:
                    via = (ratio * c + mine, 2 * base + lax.rem(big, 2))
                    slot = (big // 2) * ratio + h
                else:
                    via = (ratio * big + h, 2 * (big // 2) + odd)
                    slot = base * ratio + mine
                stays = same(goal, self.me)
                short = same(via, goal) | same(via, self.me)
                src = part(parcel.at[h], piece)
                straight = remote(
                    src, part(mirror.at[mine], piece),
                    m_send.at[piece, h], m_recv.at[piece, mine], goal,
                )
                bent = remote(
                    src, relay.at[piece, slot],
                    m_send.at[piece, h], l_recv.at[piece, slot], via,
                )
                keep = pltpu.make_async_copy(
                    src, part(mirror.at[h], piece), local.at[1 + piece]
                )
                arrival = remote(
                    src, part(mirror.at[h], piece),
                    m_send.at[piece, h], m_recv.at[piece, h], goal,
                )
                no = jnp.logical_not
                self.out.append(
                    dict(
                        goal=goal, via=via, piece=piece, h=h, stays=stays,
                        straight=no(stays) & short, bent=no(stays) & no(short),
                        straight_copy=straight, bent_copy=bent, keep=keep, arrival=arrival,
                    )
                )

        self.through = []
        relays = (big // 2) == base
        for piece in (0, 1):
            for m in range(slots):
                for k in range(ratio):
                    if piece == 0:
                        source = (ratio * (2 * m + odd) + mine, big)
                        goal = (ratio * big + k, 2 * m + odd)
                        h = k
                    else:
                        source = (ratio * big + k, 2 * m + odd)
                        goal = (ratio * (2 * m + odd) + mine, big)
                        h = mine
                    theirs = lax.rem(source[0], ratio)
                    slot = m * ratio + k
                    when = (
                        relays
                        & jnp.logical_not(same(source, self.me))
                        & jnp.logical_not(same(goal, self.me))
                        & jnp.logical_not(same(goal, source))
                    )
                    copy = remote(
                        relay.at[piece, slot], part(mirror.at[theirs], piece),
                        l_send.at[piece, slot], m_recv.at[piece, theirs], goal,
                    )
                    arrival = remote(
                        relay.at[piece, slot], relay.at[piece, slot],
                        l_send.at[piece, slot], l_recv.at[piece, slot], source,
                    )
                    self.through.append((piece, when, source, copy, arrival))

        self.into = []
        for piece in (0, 1):
            for h in range(ratio):
                source = (ratio * c + h, big)
                sb, so = source[0] // ratio, lax.rem(source[0], ratio)
                if piece == 0:
                    via = (ratio * big + so, 2 * (big // 2) + lax.rem(sb, 2))
                else:
                    via = (ratio * sb + mine, 2 * (sb // 2) + lax.rem(big, 2))
                stays = same(source, self.me)
                short = same(via, source) | same(via, self.me)
                self.into.append((source, via, stays, short))

    def greet(self, barrier, expected):
        def signal(when, to):
            @pl.when(when)
            def _():
                pl.semaphore_signal(barrier, inc=1, device_id=to, device_id_type=MESH)

        for source, via, stays, short in self.into:
            no = jnp.logical_not
            signal(no(stays) & short, source)
            signal(no(stays) & no(short), via)
        for _, when, source, _, _ in self.through:
            signal(when, source)
            expected = expected + when.astype(jnp.int32)
        for x in self.out:
            expected = expected + jnp.logical_not(x["stays"]).astype(jnp.int32)
        return expected

    def start(self):
        for x in self.out:
            pl.when(x["bent"])(x["bent_copy"].start)
        for x in self.out:
            pl.when(x["straight"])(x["straight_copy"].start)
            pl.when(x["stays"])(x["keep"].start)

    def forward(self, piece):
        for at, when, _, copy, arrival in self.through:
            if at == piece:

                @pl.when(when)
                def _():
                    arrival.wait_recv()
                    copy.start()

    def arrive(self):
        for x in self.out:
            pl.when(jnp.logical_not(x["stays"]))(x["arrival"].wait_recv)
            pl.when(x["stays"])(x["keep"].wait)

    def finish(self):
        for x in self.out:
            pl.when(jnp.logical_not(x["stays"]))(x["straight_copy"].wait_send)
        for _, when, _, copy, _ in self.through:
            pl.when(when)(copy.wait_send)


def kernel(
    n_row, n_col, tile, turned, w_taps, w_point, scale, out,
    fx, tx, sx, fl, fr, tl, tr_, sl, sr, ff, flast, tf, tlast, sf, slast,
    y0, parcel, mirror, relay, w_first, w_turned, w_second, spread,
    local, m_send, m_recv, l_send, l_recv, h_send, h_recv,
):
    r, c = lax.axis_index("row"), lax.axis_index("col")
    rows, ch, tc = tile.shape
    ratio = tc // rows
    d0, d1 = FIRST_DILATION, SECOND_DILATION

    own = pltpu.make_async_copy(tile, fx.at[pl.ds(d0, rows)], local.at[0])
    own.start()

    swap = Swap(n_row, n_col, ratio, parcel, mirror, relay, local, m_send, m_recv, l_send, l_recv)

    barrier = pltpu.get_barrier_semaphore()
    expected = jnp.int32(0)
    for dr, dc in DIRECTIONS:
        there = inside(r + dr, c + dc, n_row, n_col)
        expected = expected + there.astype(jnp.int32)

        @pl.when(there)
        def _():
            pl.semaphore_signal(
                barrier, inc=1, device_id=(r + dr, c + dc), device_id_type=MESH
            )

    expected = swap.greet(barrier, expected)

    half = rows // ratio

    @pl.loop(0, half)
    def _(j):
        for h in range(ratio):
            pair = [turned[h * rows + ratio * j + k] for k in range(ratio)]
            parcel[h, j] = jnp.concatenate(pair, axis=1)

    pl.semaphore_wait(barrier, expected)

    swap.start()

    own.wait()
    groups = rows // PACK
    f_halo = halo(fx, fl, fr, ff, flast, d0, rows, n_row, n_col, h_send.at[0], h_recv.at[0])
    start(f_halo[:2])
    pack_sides(fx, d0, ff, flast, groups, tc)
    start(f_halo[2:])
    t_halo = halo(tx, tl, tr_, tf, tlast, d0, rows, n_row, n_col, h_send.at[1], h_recv.at[1])
    s_halo = halo(sx, sl, sr, sf, slast, d1, rows, n_row, n_col, h_send.at[2], h_recv.at[2])
    clear(f_halo)
    clear(t_halo)
    clear(s_halo)
    fill_weights(w_taps, w_first, w_turned, w_second, ch)
    swap.forward(1)
    finish(f_halo)

    taps(fx, fl, fr, w_first, spread, d0, rows, tc)
    unroll = 4

    @pl.loop(0, rows // unroll)
    def _(t):
        hidden = [
            block_rows(spread, 0, t * unroll + u, d0, ch, scale, 0) for u in range(unroll)
        ]
        branch = jnp.dot(
            w_point[0], jnp.concatenate(hidden, axis=1), preferred_element_type=F32
        )
        for u in range(unroll):
            row = t * unroll + u
            y = branch[:, u * tc : (u + 1) * tc] * scale[1] + scale[3]
            y0[row] = (fx[d0 + row].astype(F32) + y).astype(BF16)

    swap.forward(0)
    swap.arrive()

    @pl.loop(0, half)
    def _(j):
        pieces = [mirror[h, j] for h in range(ratio)]
        for k in range(ratio):
            tx[d0 + ratio * j + k] = jnp.concatenate(
                [x[:, k * rows : (k + 1) * rows] for x in pieces], axis=1
            )

    start(t_halo[:2])
    pack_sides(tx, d0, tf, tlast, groups, tc)
    start(t_halo[2:])
    finish(t_halo)
    taps(tx, tl, tr_, w_turned, spread, d0, rows, tc)

    @pl.loop(0, rows // unroll)
    def _(t):
        hidden = [
            block_rows(spread, 0, t * unroll + u, d0, ch, scale, 0) for u in range(unroll)
        ]
        branch = jnp.dot(
            w_point[0], jnp.concatenate(hidden, axis=1), preferred_element_type=F32
        )
        for u in range(unroll):
            row = t * unroll + u
            y = branch[:, u * tc : (u + 1) * tc] * scale[1] + scale[3]
            y = (tx[d0 + row].astype(F32) + y).astype(BF16).astype(F32)
            sx[d1 + row] = ((y + y0[row].astype(F32)) * 0.5).astype(BF16)

    start(s_halo[:2])
    pack_sides(sx, d1, sf, slast, groups, tc)
    start(s_halo[2:])
    finish(s_halo)
    taps(sx, sl, sr, w_second, spread, d1, rows, tc)

    @pl.loop(0, rows // 2)
    def _(t):
        hidden = [
            block_rows(spread, base, t * 2 + u, d1, ch, scale, 1)
            for u in range(2)
            for base in (0, 3 * ch)
        ]
        branch = jnp.dot(
            w_point[1], jnp.concatenate(hidden, axis=1), preferred_element_type=F32
        )
        for u in range(2):
            row = t * 2 + u
            x = sx[d1 + row].astype(F32)
            both = []
            for v in (2 * u, 2 * u + 1):
                y = branch[:, v * tc : (v + 1) * tc] * scale[5] + scale[7]
                both.append((x + y).astype(BF16).astype(F32))
            out[row] = ((both[0] + both[1]) * 0.5).astype(BF16)

    swap.finish()
    finish_sends(f_halo)
    finish_sends(t_halo)
    finish_sends(s_halo)


def body(features, w_dilated, w_pointwise, norm_gain, norm_bias):
    n_row, n_col = lax.axis_size("row"), lax.axis_size("col")
    ch, rows, tc = features.shape
    ratio = tc // rows
    half = rows // ratio
    slots = ratio * (n_col // 2)
    tile = jnp.transpose(features, (1, 0, 2))
    turned = jnp.transpose(features, (2, 0, 1))
    w_taps = w_dilated.reshape(-1, ch, ch)
    scale = jnp.concatenate([norm_gain, norm_bias], axis=1).reshape(8, ch, 1)
    scale = jnp.broadcast_to(scale, (8, ch, tc))
    d0, d1 = FIRST_DILATION, SECOND_DILATION
    groups = rows // PACK

    def vmem(*shape, dtype=BF16):
        return pltpu.VMEM(shape, dtype)

    def border(d):
        return vmem(groups + 2 * d // PACK, ch, tc)

    result = pl.pallas_call(
        functools.partial(kernel, n_row, n_col),
        out_shape=jax.ShapeDtypeStruct((rows, ch, tc), BF16),
        in_specs=[pl.BlockSpec(memory_space=pl.ANY)]
        + [pl.BlockSpec(memory_space=pltpu.VMEM)] * 4,
        out_specs=pl.BlockSpec(memory_space=pltpu.VMEM),
        scratch_shapes=[
            vmem(rows + 2 * d0, ch, tc),
            vmem(rows + 2 * d0, ch, tc),
            vmem(rows + 2 * d1, ch, tc),
            border(d0), border(d0), border(d0), border(d0), border(d1), border(d1),
            *[vmem(groups, ch, tc) for _ in range(6)],
            vmem(rows, ch, tc),
            vmem(ratio, half, ch, tc),
            vmem(ratio, half, ch, tc),
            vmem(2, slots, half // 2, ch, tc),
            vmem(3 * ch, 3 * ch),
            vmem(3 * ch, 3 * ch),
            vmem(6 * ch, 3 * ch),
            vmem(rows + 2 * d1, 6 * ch, tc, dtype=F32),
            pltpu.SemaphoreType.DMA((3,)),
            pltpu.SemaphoreType.DMA((2, ratio)),
            pltpu.SemaphoreType.DMA((2, ratio)),
            pltpu.SemaphoreType.DMA((2, slots)),
            pltpu.SemaphoreType.DMA((2, slots)),
            pltpu.SemaphoreType.DMA((3, 8)),
            pltpu.SemaphoreType.DMA((3, 8)),
        ],
        compiler_params=pltpu.CompilerParams(
            collective_id=0, has_side_effects=True, vmem_limit_bytes=48 * 1024 * 1024
        ),
        cost_estimate=pl.CostEstimate(
            flops=4 * 2 * 9 * ch * ch * rows * tc, bytes_accessed=6 * ch * rows * tc, transcendentals=0
        ),
    )(tile, turned, w_taps, w_pointwise, scale)
    return jnp.transpose(result, (1, 0, 2))


def solution(mesh):
    in_specs = (P(None, "row", "col"), P(), P(), P(), P())
    out_specs = P(None, "row", "col")
    return jax.shard_map(body, mesh=mesh, in_specs=in_specs, out_specs=out_specs, check_vma=False)
```

```python
import functools

import jax
import jax.numpy as jnp
from jax import lax
from jax.experimental import pallas as pl
from jax.experimental.pallas import tpu as pltpu
from jax.sharding import PartitionSpec as P

FIRST_DILATION = 8
SECOND_DILATION = 16
SIDE = 16
PACK = 8
MESH = pl.DeviceIdType.MESH
BF16 = jnp.bfloat16
F32 = jnp.float32

DIRECTIONS = ((1, 0), (-1, 0), (0, 1), (0, -1), (1, 1), (-1, 1), (1, -1), (-1, -1))


def inside(r, c, n_row, n_col):
    return (r >= 0) & (r < n_row) & (c >= 0) & (c < n_col)


def pack_sides(main, offset, side_first, side_last, groups, tc):
    @pl.loop(0, groups)
    def _(g):
        rows = [main[offset + g * PACK + k] for k in range(PACK)]
        side_first[g] = jnp.concatenate([x[:, :SIDE] for x in rows], axis=1)
        side_last[g] = jnp.concatenate([x[:, tc - SIDE :] for x in rows], axis=1)


def halo(main, left, right, side_first, side_last, d, tr, n_row, n_col, send, recv):
    r, c = lax.axis_index("row"), lax.axis_index("col")
    hg, groups = d // PACK, tr // PACK
    moves = []
    for n, (dr, dc) in enumerate(DIRECTIONS):
        if dc == 0:
            src = main.at[pl.ds(tr, d)] if dr == 1 else main.at[pl.ds(d, d)]
            dst = main.at[pl.ds(0, d)] if dr == 1 else main.at[pl.ds(tr + d, d)]
        else:
            from_ref = side_last if dc == 1 else side_first
            to_ref = left if dc == 1 else right
            if dr == 0:
                src, dst = from_ref, to_ref.at[pl.ds(hg, groups)]
            elif dr == 1:
                src, dst = from_ref.at[pl.ds(groups - hg, hg)], to_ref.at[pl.ds(0, hg)]
            else:
                src, dst = from_ref.at[pl.ds(0, hg)], to_ref.at[pl.ds(groups + hg, hg)]
        copy = pltpu.make_async_remote_copy(
            src_ref=src,
            dst_ref=dst,
            send_sem=send.at[n],
            recv_sem=recv.at[n],
            device_id=(r + dr, c + dc),
            device_id_type=MESH,
        )
        sends = inside(r + dr, c + dc, n_row, n_col)
        receives = inside(r - dr, c - dc, n_row, n_col)
        moves.append((copy, sends, receives, dst))
    return moves


def start(moves):
    for copy, sends, _, _ in moves:
        pl.when(sends)(copy.start)


def clear(moves):
    for _, _, receives, dst in moves:

        @pl.when(jnp.logical_not(receives))
        def _():
            dst[...] = jnp.zeros(dst.shape, dst.dtype)


def finish(moves):
    for copy, _, receives, _ in moves:
        pl.when(receives)(copy.wait_recv)


def finish_sends(moves):
    for copy, sends, _, _ in moves:
        pl.when(sends)(copy.wait_send)


def shift_rows(main, lanes, first, count, d, ch, tc):
    @pl.loop(0, count // PACK)
    def _(g):
        for k in range(PACK):
            e = first + g * PACK + k
            x = jnp.maximum(main[e], jnp.zeros((), BF16))
            lanes[e, :ch] = jnp.concatenate([x[:, tc - d :], x[:, : tc - d]], axis=1)
            lanes[e, ch : 2 * ch] = x
            lanes[e, 2 * ch :] = jnp.concatenate([x[:, d:], x[:, :d]], axis=1)


def patch_sides(left, right, lanes, groups, d, ch, tc):
    @pl.loop(0, groups)
    def _(g):
        lg = jnp.maximum(left[g], jnp.zeros((), BF16))
        rg = jnp.maximum(right[g], jnp.zeros((), BF16))
        for k in range(PACK):
            at = SIDE * k
            lanes[g * PACK + k, :ch, :d] = lg[:, at + SIDE - d : at + SIDE]
            lanes[g * PACK + k, 2 * ch :, tc - d :] = rg[:, at : at + d]


def border_rows(main, left, right, lanes, rows, d, ch, tc):
    shift_rows(main, lanes, 0, d, d, ch, tc)
    shift_rows(main, lanes, rows + d, d, d, ch, tc)
    patch_sides(left, right, lanes, (rows + 2 * d) // PACK, d, ch, tc)


def hidden_rows(lanes, weights, row, count, d, ch, tc, scale, layer):
    columns = [
        jnp.concatenate([lanes[row + u + p * d] for p in range(3)], axis=0) for u in range(count)
    ]
    total = jnp.dot(
        weights[...], jnp.concatenate(columns, axis=1), preferred_element_type=F32
    )
    sets = []
    for base in range(0, weights.shape[0], ch):
        parts = [
            total[base : base + ch, u * tc : (u + 1) * tc] * scale[4 * layer]
            + scale[4 * layer + 2]
            for u in range(count)
        ]
        sets += [jnp.maximum(x, 0.0).astype(BF16) for x in parts]
    return jnp.concatenate(sets, axis=1)


def fill_weights(w_taps, w_first, w_turned, w_second, ch):
    for p in range(3):
        for q in range(3):
            at = (3 * p + q) * ch
            w_first[:, at : at + ch] = w_taps[3 * p + q]
            w_turned[:, at : at + ch] = w_taps[3 * q + p]
            w_second[:ch, at : at + ch] = w_taps[9 + 3 * p + q]
            w_second[ch:, at : at + ch] = w_taps[9 + 3 * q + p]


class Swap:
    def __init__(
        self, n_row, n_col, ratio, parcel, mirror, relay, local, m_send, m_recv, l_send, l_recv
    ):
        r, c = lax.axis_index("row"), lax.axis_index("col")
        self.me = (r, c)
        self.ratio = ratio
        self.local = local
        self.cut = parcel.shape[1] // 2
        mine = lax.rem(r, ratio)
        big = r // ratio
        odd, base = lax.rem(c, 2), c // 2
        slots = n_col // 2
        same = lambda a, b: (a[0] == b[0]) & (a[1] == b[1])
        part = lambda ref, piece: ref.at[pl.ds(piece * self.cut, self.cut)]

        def remote(src, dst, send, recv, to):
            return pltpu.make_async_remote_copy(
                src_ref=src, dst_ref=dst, send_sem=send, recv_sem=recv,
                device_id=to, device_id_type=MESH,
            )

        self.out = []
        for piece in (0, 1):
            for h in range(ratio):
                goal = (ratio * c + h, big)
                if piece == 0:
                    via = (ratio * c + mine, 2 * base + lax.rem(big, 2))
                    slot = (big // 2) * ratio + h
                else:
                    via = (ratio * big + h, 2 * (big // 2) + odd)
                    slot = base * ratio + mine
                stays = same(goal, self.me)
                short = same(via, goal) | same(via, self.me)
                src = part(parcel.at[h], piece)
                straight = remote(
                    src, part(mirror.at[mine], piece),
                    m_send.at[piece, h], m_recv.at[piece, mine], goal,
                )
                bent = remote(
                    src, relay.at[piece, slot],
                    m_send.at[piece, h], l_recv.at[piece, slot], via,
                )
                keep = pltpu.make_async_copy(
                    src, part(mirror.at[h], piece), local.at[1 + piece]
                )
                arrival = remote(
                    src, part(mirror.at[h], piece),
                    m_send.at[piece, h], m_recv.at[piece, h], goal,
                )
                no = jnp.logical_not
                self.out.append(
                    dict(
                        goal=goal, via=via, piece=piece, h=h, stays=stays,
                        straight=no(stays) & short, bent=no(stays) & no(short),
                        straight_copy=straight, bent_copy=bent, keep=keep, arrival=arrival,
                    )
                )

        self.through = []
        relays = (big // 2) == base
        for piece in (0, 1):
            for m in range(slots):
                for k in range(ratio):
                    if piece == 0:
                        source = (ratio * (2 * m + odd) + mine, big)
                        goal = (ratio * big + k, 2 * m + odd)
                        h = k
                    else:
                        source = (ratio * big + k, 2 * m + odd)
                        goal = (ratio * (2 * m + odd) + mine, big)
                        h = mine
                    theirs = lax.rem(source[0], ratio)
                    slot = m * ratio + k
                    when = (
                        relays
                        & jnp.logical_not(same(source, self.me))
                        & jnp.logical_not(same(goal, self.me))
                        & jnp.logical_not(same(goal, source))
                    )
                    copy = remote(
                        relay.at[piece, slot], part(mirror.at[theirs], piece),
                        l_send.at[piece, slot], m_recv.at[piece, theirs], goal,
                    )
                    arrival = remote(
                        relay.at[piece, slot], relay.at[piece, slot],
                        l_send.at[piece, slot], l_recv.at[piece, slot], source,
                    )
                    self.through.append((piece, when, source, copy, arrival))

        self.into = []
        for piece in (0, 1):
            for h in range(ratio):
                source = (ratio * c + h, big)
                sb, so = source[0] // ratio, lax.rem(source[0], ratio)
                if piece == 0:
                    via = (ratio * big + so, 2 * (big // 2) + lax.rem(sb, 2))
                else:
                    via = (ratio * sb + mine, 2 * (sb // 2) + lax.rem(big, 2))
                stays = same(source, self.me)
                short = same(via, source) | same(via, self.me)
                self.into.append((source, via, stays, short))

    def greet(self, barrier, expected):
        def signal(when, to):
            @pl.when(when)
            def _():
                pl.semaphore_signal(barrier, inc=1, device_id=to, device_id_type=MESH)

        for source, via, stays, short in self.into:
            no = jnp.logical_not
            signal(no(stays) & short, source)
            signal(no(stays) & no(short), via)
        for _, when, source, _, _ in self.through:
            signal(when, source)
            expected = expected + when.astype(jnp.int32)
        for x in self.out:
            expected = expected + jnp.logical_not(x["stays"]).astype(jnp.int32)
        return expected

    def start(self):
        for x in self.out:
            pl.when(x["bent"])(x["bent_copy"].start)
        for x in self.out:
            pl.when(x["straight"])(x["straight_copy"].start)
            pl.when(x["stays"])(x["keep"].start)

    def forward(self, piece):
        for at, when, _, copy, arrival in self.through:
            if at == piece:

                @pl.when(when)
                def _():
                    arrival.wait_recv()
                    copy.start()

    def arrive(self):
        for x in self.out:
            pl.when(jnp.logical_not(x["stays"]))(x["arrival"].wait_recv)
            pl.when(x["stays"])(x["keep"].wait)

    def finish(self):
        for x in self.out:
            pl.when(jnp.logical_not(x["stays"]))(x["straight_copy"].wait_send)
        for _, when, _, copy, _ in self.through:
            pl.when(when)(copy.wait_send)


def kernel(
    n_row, n_col, tile, turned, w_taps, w_point, scale, out,
    fx, tx, sx, fl, fr, tl, tr_, sl, sr, ff, flast, tf, tlast, sf, slast,
    y0, parcel, mirror, relay, w_first, w_turned, w_second, lanes,
    local, m_send, m_recv, l_send, l_recv, h_send, h_recv,
):
    r, c = lax.axis_index("row"), lax.axis_index("col")
    rows, ch, tc = tile.shape
    ratio = tc // rows
    d0, d1 = FIRST_DILATION, SECOND_DILATION

    own = pltpu.make_async_copy(tile, fx.at[pl.ds(d0, rows)], local.at[0])
    own.start()

    swap = Swap(n_row, n_col, ratio, parcel, mirror, relay, local, m_send, m_recv, l_send, l_recv)

    barrier = pltpu.get_barrier_semaphore()
    expected = jnp.int32(0)
    for dr, dc in DIRECTIONS:
        there = inside(r + dr, c + dc, n_row, n_col)
        expected = expected + there.astype(jnp.int32)

        @pl.when(there)
        def _():
            pl.semaphore_signal(
                barrier, inc=1, device_id=(r + dr, c + dc), device_id_type=MESH
            )

    expected = swap.greet(barrier, expected)

    half = rows // ratio

    @pl.loop(0, half)
    def _(j):
        for h in range(ratio):
            pair = [turned[h * rows + ratio * j + k] for k in range(ratio)]
            parcel[h, j] = jnp.concatenate(pair, axis=1)

    pl.semaphore_wait(barrier, expected)

    swap.start()

    own.wait()
    groups = rows // PACK
    f_halo = halo(fx, fl, fr, ff, flast, d0, rows, n_row, n_col, h_send.at[0], h_recv.at[0])
    start(f_halo[:2])
    pack_sides(fx, d0, ff, flast, groups, tc)
    start(f_halo[2:])
    t_halo = halo(tx, tl, tr_, tf, tlast, d0, rows, n_row, n_col, h_send.at[1], h_recv.at[1])
    s_halo = halo(sx, sl, sr, sf, slast, d1, rows, n_row, n_col, h_send.at[2], h_recv.at[2])
    clear(f_halo)
    clear(t_halo)
    clear(s_halo)
    fill_weights(w_taps, w_first, w_turned, w_second, ch)
    swap.forward(1)
    shift_rows(fx, lanes, d0, rows, d0, ch, tc)
    finish(f_halo)
    border_rows(fx, fl, fr, lanes, rows, d0, ch, tc)
    unroll = 4

    @pl.loop(0, rows // unroll)
    def _(t):
        hidden = hidden_rows(lanes, w_first, t * unroll, unroll, d0, ch, tc, scale, 0)
        branch = jnp.dot(w_point[0], hidden, preferred_element_type=F32)
        for u in range(unroll):
            row = t * unroll + u
            y = branch[:, u * tc : (u + 1) * tc] * scale[1] + scale[3]
            y0[row] = (fx[d0 + row].astype(F32) + y).astype(BF16)

    swap.forward(0)
    swap.arrive()

    @pl.loop(0, half)
    def _(j):
        pieces = [mirror[h, j] for h in range(ratio)]
        for k in range(ratio):
            tx[d0 + ratio * j + k] = jnp.concatenate(
                [x[:, k * rows : (k + 1) * rows] for x in pieces], axis=1
            )

    start(t_halo[:2])
    pack_sides(tx, d0, tf, tlast, groups, tc)
    start(t_halo[2:])
    shift_rows(tx, lanes, d0, rows, d0, ch, tc)
    finish(t_halo)
    border_rows(tx, tl, tr_, lanes, rows, d0, ch, tc)

    @pl.loop(0, rows // unroll)
    def _(t):
        hidden = hidden_rows(lanes, w_turned, t * unroll, unroll, d0, ch, tc, scale, 0)
        branch = jnp.dot(w_point[0], hidden, preferred_element_type=F32)
        for u in range(unroll):
            row = t * unroll + u
            y = branch[:, u * tc : (u + 1) * tc] * scale[1] + scale[3]
            y = (tx[d0 + row].astype(F32) + y).astype(BF16).astype(F32)
            sx[d1 + row] = ((y + y0[row].astype(F32)) * 0.5).astype(BF16)

    start(s_halo[:2])
    pack_sides(sx, d1, sf, slast, groups, tc)
    start(s_halo[2:])
    shift_rows(sx, lanes, d1, rows, d1, ch, tc)
    finish(s_halo)
    border_rows(sx, sl, sr, lanes, rows, d1, ch, tc)

    @pl.loop(0, rows // unroll)
    def _(t):
        hidden = hidden_rows(lanes, w_second, t * unroll, unroll, d1, ch, tc, scale, 1)
        branch = jnp.dot(w_point[1], hidden, preferred_element_type=F32)
        for u in range(unroll):
            row = t * unroll + u
            x = sx[d1 + row].astype(F32)
            both = []
            for v in (u, u + unroll):
                y = branch[:, v * tc : (v + 1) * tc] * scale[5] + scale[7]
                both.append((x + y).astype(BF16).astype(F32))
            out[row] = ((both[0] + both[1]) * 0.5).astype(BF16)

    swap.finish()
    finish_sends(f_halo)
    finish_sends(t_halo)
    finish_sends(s_halo)


def body(features, w_dilated, w_pointwise, norm_gain, norm_bias):
    n_row, n_col = lax.axis_size("row"), lax.axis_size("col")
    ch, rows, tc = features.shape
    ratio = tc // rows
    half = rows // ratio
    slots = ratio * (n_col // 2)
    tile = jnp.transpose(features, (1, 0, 2))
    turned = jnp.transpose(features, (2, 0, 1))
    w_taps = w_dilated.reshape(-1, ch, ch)
    scale = jnp.concatenate([norm_gain, norm_bias], axis=1).reshape(8, ch, 1)
    scale = jnp.broadcast_to(scale, (8, ch, tc))
    d0, d1 = FIRST_DILATION, SECOND_DILATION
    groups = rows // PACK

    def vmem(*shape, dtype=BF16):
        return pltpu.VMEM(shape, dtype)

    def border(d):
        return vmem(groups + 2 * d // PACK, ch, tc)

    result = pl.pallas_call(
        functools.partial(kernel, n_row, n_col),
        out_shape=jax.ShapeDtypeStruct((rows, ch, tc), BF16),
        in_specs=[pl.BlockSpec(memory_space=pl.ANY)]
        + [pl.BlockSpec(memory_space=pltpu.VMEM)] * 4,
        out_specs=pl.BlockSpec(memory_space=pltpu.VMEM),
        scratch_shapes=[
            vmem(rows + 2 * d0, ch, tc),
            vmem(rows + 2 * d0, ch, tc),
            vmem(rows + 2 * d1, ch, tc),
            border(d0), border(d0), border(d0), border(d0), border(d1), border(d1),
            *[vmem(groups, ch, tc) for _ in range(6)],
            vmem(rows, ch, tc),
            vmem(ratio, half, ch, tc),
            vmem(ratio, half, ch, tc),
            vmem(2, slots, half // 2, ch, tc),
            vmem(ch, 9 * ch),
            vmem(ch, 9 * ch),
            vmem(2 * ch, 9 * ch),
            vmem(rows + 2 * d1, 3 * ch, tc),
            pltpu.SemaphoreType.DMA((3,)),
            pltpu.SemaphoreType.DMA((2, ratio)),
            pltpu.SemaphoreType.DMA((2, ratio)),
            pltpu.SemaphoreType.DMA((2, slots)),
            pltpu.SemaphoreType.DMA((2, slots)),
            pltpu.SemaphoreType.DMA((3, 8)),
            pltpu.SemaphoreType.DMA((3, 8)),
        ],
        compiler_params=pltpu.CompilerParams(
            collective_id=0, has_side_effects=True, vmem_limit_bytes=48 * 1024 * 1024
        ),
        cost_estimate=pl.CostEstimate(
            flops=4 * 2 * 9 * ch * ch * rows * tc, bytes_accessed=6 * ch * rows * tc, transcendentals=0
        ),
    )(tile, turned, w_taps, w_pointwise, scale)
    return jnp.transpose(result, (1, 0, 2))


def solution(mesh):
    in_specs = (P(None, "row", "col"), P(), P(), P(), P())
    out_specs = P(None, "row", "col")
    return jax.shard_map(body, mesh=mesh, in_specs=in_specs, out_specs=out_specs, check_vma=False)
```

```python
import functools

import jax
import jax.numpy as jnp
from jax import lax
from jax.experimental import pallas as pl
from jax.experimental.pallas import tpu as pltpu
from jax.sharding import PartitionSpec as P

FIRST_DILATION = 8
SECOND_DILATION = 16
SIDE = 16
PACK = 8
MESH = pl.DeviceIdType.MESH
BF16 = jnp.bfloat16
F32 = jnp.float32

DIRECTIONS = ((1, 0), (-1, 0), (0, 1), (0, -1), (1, 1), (-1, 1), (1, -1), (-1, -1))


def inside(r, c, n_row, n_col):
    return (r >= 0) & (r < n_row) & (c >= 0) & (c < n_col)


def pack_sides(main, offset, side_first, side_last, groups, tc):
    @pl.loop(0, groups)
    def _(g):
        rows = [main[offset + g * PACK + k] for k in range(PACK)]
        side_first[g] = jnp.concatenate([x[:, :SIDE] for x in rows], axis=1)
        side_last[g] = jnp.concatenate([x[:, tc - SIDE :] for x in rows], axis=1)


def halo(main, left, right, side_first, side_last, d, tr, n_row, n_col, send, recv):
    r, c = lax.axis_index("row"), lax.axis_index("col")
    hg, groups = d // PACK, tr // PACK
    moves = []
    for n, (dr, dc) in enumerate(DIRECTIONS):
        if dc == 0:
            src = main.at[pl.ds(tr, d)] if dr == 1 else main.at[pl.ds(d, d)]
            dst = main.at[pl.ds(0, d)] if dr == 1 else main.at[pl.ds(tr + d, d)]
        else:
            from_ref = side_last if dc == 1 else side_first
            to_ref = left if dc == 1 else right
            if dr == 0:
                src, dst = from_ref, to_ref.at[pl.ds(hg, groups)]
            elif dr == 1:
                src, dst = from_ref.at[pl.ds(groups - hg, hg)], to_ref.at[pl.ds(0, hg)]
            else:
                src, dst = from_ref.at[pl.ds(0, hg)], to_ref.at[pl.ds(groups + hg, hg)]
        copy = pltpu.make_async_remote_copy(
            src_ref=src,
            dst_ref=dst,
            send_sem=send.at[n],
            recv_sem=recv.at[n],
            device_id=(r + dr, c + dc),
            device_id_type=MESH,
        )
        sends = inside(r + dr, c + dc, n_row, n_col)
        receives = inside(r - dr, c - dc, n_row, n_col)
        moves.append((copy, sends, receives, dst))
    return moves


def start(moves):
    for copy, sends, _, _ in moves:
        pl.when(sends)(copy.start)


def clear(moves):
    for _, _, receives, dst in moves:

        @pl.when(jnp.logical_not(receives))
        def _():
            dst[...] = jnp.zeros(dst.shape, dst.dtype)


def finish(moves):
    for copy, _, receives, _ in moves:
        pl.when(receives)(copy.wait_recv)


def finish_sends(moves):
    for copy, sends, _, _ in moves:
        pl.when(sends)(copy.wait_send)


def shift_rows(main, lanes, first, count, d, ch, tc):
    @pl.loop(0, count // PACK)
    def _(g):
        for k in range(PACK):
            e = first + g * PACK + k
            x = jnp.maximum(main[e], jnp.zeros((), BF16))
            lanes[e, :ch] = jnp.concatenate([x[:, tc - d :], x[:, : tc - d]], axis=1)
            lanes[e, ch : 2 * ch] = x
            lanes[e, 2 * ch :] = jnp.concatenate([x[:, d:], x[:, :d]], axis=1)


def patch_sides(left, right, lanes, groups, d, ch, tc):
    @pl.loop(0, groups)
    def _(g):
        lg = jnp.maximum(left[g], jnp.zeros((), BF16))
        rg = jnp.maximum(right[g], jnp.zeros((), BF16))
        for k in range(PACK):
            at = SIDE * k
            lanes[g * PACK + k, :ch, :d] = lg[:, at + SIDE - d : at + SIDE]
            lanes[g * PACK + k, 2 * ch :, tc - d :] = rg[:, at : at + d]


def border_rows(main, left, right, lanes, rows, d, ch, tc):
    shift_rows(main, lanes, 0, d, d, ch, tc)
    shift_rows(main, lanes, rows + d, d, d, ch, tc)
    patch_sides(left, right, lanes, (rows + 2 * d) // PACK, d, ch, tc)


def hidden_rows(lanes, weights, row, count, d, ch, tc, scale, layer):
    columns = [
        jnp.concatenate([lanes[row + u + p * d] for p in range(3)], axis=0) for u in range(count)
    ]
    total = jnp.dot(
        weights[...], jnp.concatenate(columns, axis=1), preferred_element_type=F32
    )
    sets = []
    for base in range(0, weights.shape[0], ch):
        parts = [
            total[base : base + ch, u * tc : (u + 1) * tc] * scale[4 * layer]
            + scale[4 * layer + 2]
            for u in range(count)
        ]
        sets += [jnp.maximum(x, 0.0).astype(BF16) for x in parts]
    return jnp.concatenate(sets, axis=1)


def fill_weights(w_taps, w_first, w_turned, w_second, ch):
    for p in range(3):
        for q in range(3):
            at = (3 * p + q) * ch
            w_first[:, at : at + ch] = w_taps[3 * p + q]
            w_turned[:, at : at + ch] = w_taps[3 * q + p]
            w_second[:ch, at : at + ch] = w_taps[9 + 3 * p + q]
            w_second[ch:, at : at + ch] = w_taps[9 + 3 * q + p]


class Swap:
    def __init__(
        self, n_row, n_col, ratio, parcel, mirror, relay, local, m_send, m_recv, l_send, l_recv
    ):
        r, c = lax.axis_index("row"), lax.axis_index("col")
        self.me = (r, c)
        self.ratio = ratio
        self.local = local
        self.cut = parcel.shape[1] // 2
        mine = lax.rem(r, ratio)
        big = r // ratio
        odd, base = lax.rem(c, 2), c // 2
        slots = n_col // 2
        same = lambda a, b: (a[0] == b[0]) & (a[1] == b[1])
        part = lambda ref, piece: ref.at[pl.ds(piece * self.cut, self.cut)]

        def remote(src, dst, send, recv, to):
            return pltpu.make_async_remote_copy(
                src_ref=src, dst_ref=dst, send_sem=send, recv_sem=recv,
                device_id=to, device_id_type=MESH,
            )

        self.out = []
        for piece in (0, 1):
            for h in range(ratio):
                goal = (ratio * c + h, big)
                if piece == 0:
                    via = (ratio * c + mine, 2 * base + lax.rem(big, 2))
                    slot = (big // 2) * ratio + h
                else:
                    via = (ratio * big + h, 2 * (big // 2) + odd)
                    slot = base * ratio + mine
                stays = same(goal, self.me)
                short = same(via, goal) | same(via, self.me)
                src = part(parcel.at[h], piece)
                straight = remote(
                    src, part(mirror.at[mine], piece),
                    m_send.at[piece, h], m_recv.at[piece, mine], goal,
                )
                bent = remote(
                    src, relay.at[piece, slot],
                    m_send.at[piece, h], l_recv.at[piece, slot], via,
                )
                keep = pltpu.make_async_copy(
                    src, part(mirror.at[h], piece), local.at[1 + piece]
                )
                arrival = remote(
                    src, part(mirror.at[h], piece),
                    m_send.at[piece, h], m_recv.at[piece, h], goal,
                )
                no = jnp.logical_not
                self.out.append(
                    dict(
                        goal=goal, via=via, piece=piece, h=h, stays=stays,
                        straight=no(stays) & short, bent=no(stays) & no(short),
                        straight_copy=straight, bent_copy=bent, keep=keep, arrival=arrival,
                    )
                )

        self.through = []
        relays = (big // 2) == base
        for piece in (0, 1):
            for m in range(slots):
                for k in range(ratio):
                    if piece == 0:
                        source = (ratio * (2 * m + odd) + mine, big)
                        goal = (ratio * big + k, 2 * m + odd)
                        h = k
                    else:
                        source = (ratio * big + k, 2 * m + odd)
                        goal = (ratio * (2 * m + odd) + mine, big)
                        h = mine
                    theirs = lax.rem(source[0], ratio)
                    slot = m * ratio + k
                    when = (
                        relays
                        & jnp.logical_not(same(source, self.me))
                        & jnp.logical_not(same(goal, self.me))
                        & jnp.logical_not(same(goal, source))
                    )
                    copy = remote(
                        relay.at[piece, slot], part(mirror.at[theirs], piece),
                        l_send.at[piece, slot], m_recv.at[piece, theirs], goal,
                    )
                    arrival = remote(
                        relay.at[piece, slot], relay.at[piece, slot],
                        l_send.at[piece, slot], l_recv.at[piece, slot], source,
                    )
                    self.through.append((piece, when, source, copy, arrival))

        self.into = []
        for piece in (0, 1):
            for h in range(ratio):
                source = (ratio * c + h, big)
                sb, so = source[0] // ratio, lax.rem(source[0], ratio)
                if piece == 0:
                    via = (ratio * big + so, 2 * (big // 2) + lax.rem(sb, 2))
                else:
                    via = (ratio * sb + mine, 2 * (sb // 2) + lax.rem(big, 2))
                stays = same(source, self.me)
                short = same(via, source) | same(via, self.me)
                self.into.append((source, via, stays, short))

    def greet(self, barrier, expected):
        def signal(when, to):
            @pl.when(when)
            def _():
                pl.semaphore_signal(barrier, inc=1, device_id=to, device_id_type=MESH)

        for source, via, stays, short in self.into:
            no = jnp.logical_not
            signal(no(stays) & short, source)
            signal(no(stays) & no(short), via)
        for _, when, source, _, _ in self.through:
            signal(when, source)
            expected = expected + when.astype(jnp.int32)
        for x in self.out:
            expected = expected + jnp.logical_not(x["stays"]).astype(jnp.int32)
        return expected

    def start(self):
        for x in self.out:
            pl.when(x["bent"])(x["bent_copy"].start)
        for x in self.out:
            pl.when(x["straight"])(x["straight_copy"].start)
            pl.when(x["stays"])(x["keep"].start)

    def forward(self, piece, turn, turns):
        passing = [x for x in self.through if x[0] == piece]
        share = -(-len(passing) // turns)
        for _, when, _, copy, arrival in passing[turn * share : (turn + 1) * share]:

            @pl.when(when)
            def _():
                arrival.wait_recv()
                copy.start()

    def arrive(self):
        for x in self.out:
            pl.when(jnp.logical_not(x["stays"]))(x["arrival"].wait_recv)
            pl.when(x["stays"])(x["keep"].wait)

    def finish(self):
        for x in self.out:
            pl.when(jnp.logical_not(x["stays"]))(x["straight_copy"].wait_send)
        for _, when, _, copy, _ in self.through:
            pl.when(when)(copy.wait_send)


def kernel(
    n_row, n_col, tile, turned, w_taps, w_point, gain, bias, out,
    fx, tx, sx, fl, fr, tl, tr_, sl, sr, ff, flast, tf, tlast, sf, slast,
    y0, parcel, mirror, relay, w_first, w_turned, w_second, lanes, scale,
    local, m_send, m_recv, l_send, l_recv, h_send, h_recv,
):
    r, c = lax.axis_index("row"), lax.axis_index("col")
    rows, ch, tc = tile.shape
    ratio = tc // rows
    d0, d1 = FIRST_DILATION, SECOND_DILATION

    own = pltpu.make_async_copy(tile, fx.at[pl.ds(d0, rows)], local.at[0])
    own.start()

    swap = Swap(n_row, n_col, ratio, parcel, mirror, relay, local, m_send, m_recv, l_send, l_recv)

    barrier = pltpu.get_barrier_semaphore()
    expected = jnp.int32(0)
    for dr, dc in DIRECTIONS:
        there = inside(r + dr, c + dc, n_row, n_col)
        expected = expected + there.astype(jnp.int32)

        @pl.when(there)
        def _():
            pl.semaphore_signal(
                barrier, inc=1, device_id=(r + dr, c + dc), device_id_type=MESH
            )

    expected = swap.greet(barrier, expected)

    half = rows // ratio
    groups = rows // PACK

    @pl.loop(0, half)
    def _(j):
        for h in range(ratio):
            pair = [turned[h * rows + ratio * j + k] for k in range(ratio)]
            parcel[h, j] = jnp.concatenate(pair, axis=1)

    own.wait()
    pack_sides(fx, d0, ff, flast, groups, tc)
    f_halo = halo(fx, fl, fr, ff, flast, d0, rows, n_row, n_col, h_send.at[0], h_recv.at[0])
    pl.semaphore_wait(barrier, expected)

    start(f_halo)
    swap.start()

    t_halo = halo(tx, tl, tr_, tf, tlast, d0, rows, n_row, n_col, h_send.at[1], h_recv.at[1])
    s_halo = halo(sx, sl, sr, sf, slast, d1, rows, n_row, n_col, h_send.at[2], h_recv.at[2])
    clear(f_halo)
    clear(t_halo)
    clear(s_halo)
    fill_weights(w_taps, w_first, w_turned, w_second, ch)
    for layer in range(2):
        for n in range(2):
            for at, ref in ((0, gain), (2, bias)):
                line = jnp.broadcast_to(ref[layer, n : n + 1, :], (tc, ch))
                scale[4 * layer + at + n] = line.T
    swap.forward(1, 0, 1)
    shift_rows(fx, lanes, d0, rows, d0, ch, tc)
    finish(f_halo)
    border_rows(fx, fl, fr, lanes, rows, d0, ch, tc)
    unroll = 4
    steps = rows // unroll
    turns = 4
    for turn in range(turns):

        @pl.loop(turn * steps // turns, (turn + 1) * steps // turns)
        def _(t):
            hidden = hidden_rows(lanes, w_first, t * unroll, unroll, d0, ch, tc, scale, 0)
            branch = jnp.dot(w_point[0], hidden, preferred_element_type=F32)
            for u in range(unroll):
                row = t * unroll + u
                y = branch[:, u * tc : (u + 1) * tc] * scale[1] + scale[3]
                y0[row] = (fx[d0 + row].astype(F32) + y).astype(BF16)

        swap.forward(0, turn, turns)

    swap.arrive()

    @pl.loop(0, half)
    def _(j):
        pieces = [mirror[h, j] for h in range(ratio)]
        for k in range(ratio):
            tx[d0 + ratio * j + k] = jnp.concatenate(
                [x[:, k * rows : (k + 1) * rows] for x in pieces], axis=1
            )

    start(t_halo[:2])
    pack_sides(tx, d0, tf, tlast, groups, tc)
    start(t_halo[2:])
    shift_rows(tx, lanes, d0, rows, d0, ch, tc)
    finish(t_halo)
    border_rows(tx, tl, tr_, lanes, rows, d0, ch, tc)

    @pl.loop(0, rows // unroll)
    def _(t):
        hidden = hidden_rows(lanes, w_turned, t * unroll, unroll, d0, ch, tc, scale, 0)
        branch = jnp.dot(w_point[0], hidden, preferred_element_type=F32)
        for u in range(unroll):
            row = t * unroll + u
            y = branch[:, u * tc : (u + 1) * tc] * scale[1] + scale[3]
            y = (tx[d0 + row].astype(F32) + y).astype(BF16).astype(F32)
            sx[d1 + row] = ((y + y0[row].astype(F32)) * 0.5).astype(BF16)

    start(s_halo[:2])
    pack_sides(sx, d1, sf, slast, groups, tc)
    start(s_halo[2:])
    shift_rows(sx, lanes, d1, rows, d1, ch, tc)
    finish(s_halo)
    border_rows(sx, sl, sr, lanes, rows, d1, ch, tc)

    @pl.loop(0, rows // unroll)
    def _(t):
        hidden = hidden_rows(lanes, w_second, t * unroll, unroll, d1, ch, tc, scale, 1)
        branch = jnp.dot(w_point[1], hidden, preferred_element_type=F32)
        for u in range(unroll):
            row = t * unroll + u
            x = sx[d1 + row].astype(F32)
            both = []
            for v in (u, u + unroll):
                y = branch[:, v * tc : (v + 1) * tc] * scale[5] + scale[7]
                both.append((x + y).astype(BF16).astype(F32))
            out[row] = ((both[0] + both[1]) * 0.5).astype(BF16)

    swap.finish()
    finish_sends(f_halo)
    finish_sends(t_halo)
    finish_sends(s_halo)


def body(features, w_dilated, w_pointwise, norm_gain, norm_bias):
    n_row, n_col = lax.axis_size("row"), lax.axis_size("col")
    ch, rows, tc = features.shape
    ratio = tc // rows
    half = rows // ratio
    slots = ratio * (n_col // 2)
    tile = jnp.transpose(features, (1, 0, 2))
    turned = jnp.transpose(features, (2, 0, 1))
    w_taps = w_dilated.reshape(-1, ch, ch)
    d0, d1 = FIRST_DILATION, SECOND_DILATION
    groups = rows // PACK

    def vmem(*shape, dtype=BF16):
        return pltpu.VMEM(shape, dtype)

    def border(d):
        return vmem(groups + 2 * d // PACK, ch, tc)

    result = pl.pallas_call(
        functools.partial(kernel, n_row, n_col),
        out_shape=jax.ShapeDtypeStruct((rows, ch, tc), BF16),
        in_specs=[pl.BlockSpec(memory_space=pltpu.VMEM)] * 6,
        out_specs=pl.BlockSpec(memory_space=pltpu.VMEM),
        scratch_shapes=[
            vmem(rows + 2 * d0, ch, tc),
            vmem(rows + 2 * d0, ch, tc),
            vmem(rows + 2 * d1, ch, tc),
            border(d0), border(d0), border(d0), border(d0), border(d1), border(d1),
            *[vmem(groups, ch, tc) for _ in range(6)],
            vmem(rows, ch, tc),
            vmem(ratio, half, ch, tc),
            vmem(ratio, half, ch, tc),
            vmem(2, slots, half // 2, ch, tc),
            vmem(ch, 9 * ch),
            vmem(ch, 9 * ch),
            vmem(2 * ch, 9 * ch),
            vmem(rows + 2 * d1, 3 * ch, tc),
            vmem(8, ch, tc, dtype=F32),
            pltpu.SemaphoreType.DMA((3,)),
            pltpu.SemaphoreType.DMA((2, ratio)),
            pltpu.SemaphoreType.DMA((2, ratio)),
            pltpu.SemaphoreType.DMA((2, slots)),
            pltpu.SemaphoreType.DMA((2, slots)),
            pltpu.SemaphoreType.DMA((3, 8)),
            pltpu.SemaphoreType.DMA((3, 8)),
        ],
        compiler_params=pltpu.CompilerParams(
            collective_id=0, has_side_effects=True, vmem_limit_bytes=48 * 1024 * 1024
        ),
        cost_estimate=pl.CostEstimate(
            flops=4 * 2 * 9 * ch * ch * rows * tc, bytes_accessed=6 * ch * rows * tc, transcendentals=0
        ),
    )(tile, turned, w_taps, w_pointwise, norm_gain, norm_bias)
    return jnp.transpose(result, (1, 0, 2))


def solution(mesh):
    in_specs = (P(None, "row", "col"), P(), P(), P(), P())
    out_specs = P(None, "row", "col")
    return jax.shard_map(body, mesh=mesh, in_specs=in_specs, out_specs=out_specs, check_vma=False)
```

```python
import functools

import jax
import jax.numpy as jnp
from jax import lax
from jax.experimental import pallas as pl
from jax.experimental.pallas import tpu as pltpu
from jax.sharding import PartitionSpec as P

FIRST_DILATION = 8
SECOND_DILATION = 16
SIDE = 16
PACK = 8
MESH = pl.DeviceIdType.MESH
BF16 = jnp.bfloat16
F32 = jnp.float32

DIRECTIONS = ((1, 0), (-1, 0), (0, 1), (0, -1), (1, 1), (-1, 1), (1, -1), (-1, -1))


def inside(r, c, n_row, n_col):
    return (r >= 0) & (r < n_row) & (c >= 0) & (c < n_col)


def pack_sides(main, offset, side_first, side_last, groups, tc):
    @pl.loop(0, groups)
    def _(g):
        rows = [main[offset + g * PACK + k] for k in range(PACK)]
        side_first[g] = jnp.concatenate([x[:, :SIDE] for x in rows], axis=1)
        side_last[g] = jnp.concatenate([x[:, tc - SIDE :] for x in rows], axis=1)


def halo(main, left, right, side_first, side_last, d, tr, n_row, n_col, send, recv):
    r, c = lax.axis_index("row"), lax.axis_index("col")
    hg, groups = d // PACK, tr // PACK
    moves = []
    for n, (dr, dc) in enumerate(DIRECTIONS):
        if dc == 0:
            src = main.at[pl.ds(tr, d)] if dr == 1 else main.at[pl.ds(d, d)]
            dst = main.at[pl.ds(0, d)] if dr == 1 else main.at[pl.ds(tr + d, d)]
        else:
            from_ref = side_last if dc == 1 else side_first
            to_ref = left if dc == 1 else right
            if dr == 0:
                src, dst = from_ref, to_ref.at[pl.ds(hg, groups)]
            elif dr == 1:
                src, dst = from_ref.at[pl.ds(groups - hg, hg)], to_ref.at[pl.ds(0, hg)]
            else:
                src, dst = from_ref.at[pl.ds(0, hg)], to_ref.at[pl.ds(groups + hg, hg)]
        copy = pltpu.make_async_remote_copy(
            src_ref=src,
            dst_ref=dst,
            send_sem=send.at[n],
            recv_sem=recv.at[n],
            device_id=(r + dr, c + dc),
            device_id_type=MESH,
        )
        sends = inside(r + dr, c + dc, n_row, n_col)
        receives = inside(r - dr, c - dc, n_row, n_col)
        moves.append((copy, sends, receives, dst))
    return moves


def start(moves):
    for copy, sends, _, _ in moves:
        pl.when(sends)(copy.start)


def clear(moves):
    for _, _, receives, dst in moves:

        @pl.when(jnp.logical_not(receives))
        def _():
            dst[...] = jnp.zeros(dst.shape, dst.dtype)


def finish(moves):
    for copy, _, receives, _ in moves:
        pl.when(receives)(copy.wait_recv)


def finish_sends(moves):
    for copy, sends, _, _ in moves:
        pl.when(sends)(copy.wait_send)


def shift_rows(main, lanes, first, count, d, ch, tc):
    @pl.loop(0, count // PACK)
    def _(g):
        for k in range(PACK):
            e = first + g * PACK + k
            x = jnp.maximum(main[e], jnp.zeros((), BF16))
            lanes[e, :ch] = jnp.concatenate([x[:, tc - d :], x[:, : tc - d]], axis=1)
            lanes[e, ch : 2 * ch] = x
            lanes[e, 2 * ch :] = jnp.concatenate([x[:, d:], x[:, :d]], axis=1)


def patch_sides(left, right, lanes, first, last, d, ch, tc):
    @pl.loop(first, last)
    def _(g):
        lg = jnp.maximum(left[g], jnp.zeros((), BF16))
        rg = jnp.maximum(right[g], jnp.zeros((), BF16))
        for k in range(PACK):
            at = SIDE * k
            lanes[g * PACK + k, :ch, :d] = lg[:, at + SIDE - d : at + SIDE]
            lanes[g * PACK + k, 2 * ch :, tc - d :] = rg[:, at : at + d]


def border_rows(main, left, right, lanes, rows, d, ch, tc):
    shift_rows(main, lanes, 0, d, d, ch, tc)
    shift_rows(main, lanes, rows + d, d, d, ch, tc)
    hg, groups = d // PACK, rows // PACK
    patch_sides(left, right, lanes, 0, hg, d, ch, tc)
    patch_sides(left, right, lanes, hg + groups, 2 * hg + groups, d, ch, tc)


def own_sides(left, right, lanes, rows, d, ch, tc):
    first = d // PACK
    patch_sides(left, right, lanes, first, first + rows // PACK, d, ch, tc)


def hidden_rows(lanes, weights, row, count, d, ch, tc, scale, layer):
    columns = [
        jnp.concatenate([lanes[row + u + p * d] for p in range(3)], axis=0) for u in range(count)
    ]
    total = jnp.dot(
        weights[...], jnp.concatenate(columns, axis=1), preferred_element_type=F32
    )
    sets = []
    for base in range(0, weights.shape[0], ch):
        parts = [
            total[base : base + ch, u * tc : (u + 1) * tc] * scale[4 * layer]
            + scale[4 * layer + 2]
            for u in range(count)
        ]
        sets += [jnp.maximum(x, 0.0).astype(BF16) for x in parts]
    return jnp.concatenate(sets, axis=1)


def fill_weights(w_taps, w_first, w_turned, w_second, ch):
    for p in range(3):
        for q in range(3):
            at = (3 * p + q) * ch
            w_first[:, at : at + ch] = w_taps[3 * p + q]
            w_turned[:, at : at + ch] = w_taps[3 * q + p]
            w_second[:ch, at : at + ch] = w_taps[9 + 3 * p + q]
            w_second[ch:, at : at + ch] = w_taps[9 + 3 * q + p]


class Swap:
    def __init__(
        self, n_row, n_col, ratio, parcel, mirror, relay, local, m_send, m_recv, l_send, l_recv
    ):
        r, c = lax.axis_index("row"), lax.axis_index("col")
        self.me = (r, c)
        self.ratio = ratio
        self.local = local
        self.cut = parcel.shape[1] // 2
        mine = lax.rem(r, ratio)
        big = r // ratio
        odd, base = lax.rem(c, 2), c // 2
        slots = n_col // 2
        same = lambda a, b: (a[0] == b[0]) & (a[1] == b[1])
        part = lambda ref, piece: ref.at[pl.ds(piece * self.cut, self.cut)]

        def remote(src, dst, send, recv, to):
            return pltpu.make_async_remote_copy(
                src_ref=src, dst_ref=dst, send_sem=send, recv_sem=recv,
                device_id=to, device_id_type=MESH,
            )

        self.out = []
        for piece in (0, 1):
            for h in range(ratio):
                goal = (ratio * c + h, big)
                if piece == 0:
                    via = (ratio * c + mine, 2 * base + lax.rem(big, 2))
                    slot = (big // 2) * ratio + h
                else:
                    via = (ratio * big + h, 2 * (big // 2) + odd)
                    slot = base * ratio + mine
                stays = same(goal, self.me)
                short = same(via, goal) | same(via, self.me)
                src = part(parcel.at[h], piece)
                straight = remote(
                    src, part(mirror.at[mine], piece),
                    m_send.at[piece, h], m_recv.at[piece, mine], goal,
                )
                bent = remote(
                    src, relay.at[piece, slot],
                    m_send.at[piece, h], l_recv.at[piece, slot], via,
                )
                keep = pltpu.make_async_copy(
                    src, part(mirror.at[h], piece), local.at[1 + piece]
                )
                arrival = remote(
                    src, part(mirror.at[h], piece),
                    m_send.at[piece, h], m_recv.at[piece, h], goal,
                )
                no = jnp.logical_not
                self.out.append(
                    dict(
                        goal=goal, via=via, piece=piece, h=h, stays=stays,
                        straight=no(stays) & short, bent=no(stays) & no(short),
                        straight_copy=straight, bent_copy=bent, keep=keep, arrival=arrival,
                    )
                )

        self.through = []
        relays = (big // 2) == base
        for piece in (0, 1):
            for m in range(slots):
                for k in range(ratio):
                    if piece == 0:
                        source = (ratio * (2 * m + odd) + mine, big)
                        goal = (ratio * big + k, 2 * m + odd)
                        h = k
                    else:
                        source = (ratio * big + k, 2 * m + odd)
                        goal = (ratio * (2 * m + odd) + mine, big)
                        h = mine
                    theirs = lax.rem(source[0], ratio)
                    slot = m * ratio + k
                    when = (
                        relays
                        & jnp.logical_not(same(source, self.me))
                        & jnp.logical_not(same(goal, self.me))
                        & jnp.logical_not(same(goal, source))
                    )
                    copy = remote(
                        relay.at[piece, slot], part(mirror.at[theirs], piece),
                        l_send.at[piece, slot], m_recv.at[piece, theirs], goal,
                    )
                    arrival = remote(
                        relay.at[piece, slot], relay.at[piece, slot],
                        l_send.at[piece, slot], l_recv.at[piece, slot], source,
                    )
                    self.through.append((piece, when, source, copy, arrival))

        self.into = []
        for piece in (0, 1):
            for h in range(ratio):
                source = (ratio * c + h, big)
                sb, so = source[0] // ratio, lax.rem(source[0], ratio)
                if piece == 0:
                    via = (ratio * big + so, 2 * (big // 2) + lax.rem(sb, 2))
                else:
                    via = (ratio * sb + mine, 2 * (sb // 2) + lax.rem(big, 2))
                stays = same(source, self.me)
                short = same(via, source) | same(via, self.me)
                self.into.append((source, via, stays, short))

    def greet(self, barrier, expected):
        def signal(when, to):
            @pl.when(when)
            def _():
                pl.semaphore_signal(barrier, inc=1, device_id=to, device_id_type=MESH)

        for source, via, stays, short in self.into:
            no = jnp.logical_not
            signal(no(stays) & short, source)
            signal(no(stays) & no(short), via)
        for _, when, source, _, _ in self.through:
            signal(when, source)
            expected = expected + when.astype(jnp.int32)
        for x in self.out:
            expected = expected + jnp.logical_not(x["stays"]).astype(jnp.int32)
        return expected

    def start(self):
        for x in self.out:
            pl.when(x["bent"])(x["bent_copy"].start)
        for x in self.out:
            pl.when(x["straight"])(x["straight_copy"].start)
            pl.when(x["stays"])(x["keep"].start)

    def forward(self, piece, turn, turns):
        passing = [x for x in self.through if x[0] == piece]
        share = -(-len(passing) // turns)
        for _, when, _, copy, arrival in passing[turn * share : (turn + 1) * share]:

            @pl.when(when)
            def _():
                arrival.wait_recv()
                copy.start()

    def arrive(self, piece):
        for x in self.out[piece * self.ratio : (piece + 1) * self.ratio]:
            pl.when(jnp.logical_not(x["stays"]))(x["arrival"].wait_recv)
            pl.when(x["stays"])(x["keep"].wait)

    def finish(self):
        for x in self.out:
            pl.when(jnp.logical_not(x["stays"]))(x["straight_copy"].wait_send)
        for _, when, _, copy, _ in self.through:
            pl.when(when)(copy.wait_send)


def kernel(
    n_row, n_col, tile, turned, w_taps, w_point, gain, bias, out,
    fx, tx, sx, fl, fr, tl, tr_, sl, sr, ff, flast, tf, tlast, sf, slast,
    y0, parcel, mirror, relay, w_first, w_turned, w_second, lanes, scale,
    local, m_send, m_recv, l_send, l_recv, h_send, h_recv,
):
    r, c = lax.axis_index("row"), lax.axis_index("col")
    rows, ch, tc = tile.shape
    ratio = tc // rows
    d0, d1 = FIRST_DILATION, SECOND_DILATION

    own = pltpu.make_async_copy(tile, fx.at[pl.ds(d0, rows)], local.at[0])
    own.start()

    swap = Swap(n_row, n_col, ratio, parcel, mirror, relay, local, m_send, m_recv, l_send, l_recv)

    barrier = pltpu.get_barrier_semaphore()
    expected = jnp.int32(0)
    for dr, dc in DIRECTIONS:
        there = inside(r + dr, c + dc, n_row, n_col)
        expected = expected + there.astype(jnp.int32)

        @pl.when(there)
        def _():
            pl.semaphore_signal(
                barrier, inc=1, device_id=(r + dr, c + dc), device_id_type=MESH
            )

    expected = swap.greet(barrier, expected)

    half = rows // ratio
    groups = rows // PACK

    @pl.loop(0, half)
    def _(j):
        for h in range(ratio):
            pair = [turned[h * rows + ratio * j + k] for k in range(ratio)]
            parcel[h, j] = jnp.concatenate(pair, axis=1)

    own.wait()
    pack_sides(fx, d0, ff, flast, groups, tc)
    f_halo = halo(fx, fl, fr, ff, flast, d0, rows, n_row, n_col, h_send.at[0], h_recv.at[0])
    pl.semaphore_wait(barrier, expected)

    start(f_halo)
    swap.start()

    t_halo = halo(tx, tl, tr_, tf, tlast, d0, rows, n_row, n_col, h_send.at[1], h_recv.at[1])
    s_halo = halo(sx, sl, sr, sf, slast, d1, rows, n_row, n_col, h_send.at[2], h_recv.at[2])
    clear(f_halo)
    clear(t_halo)
    clear(s_halo)
    fill_weights(w_taps, w_first, w_turned, w_second, ch)
    for layer in range(2):
        for n in range(2):
            for at, ref in ((0, gain), (2, bias)):
                line = jnp.broadcast_to(ref[layer, n : n + 1, :], (tc, ch))
                scale[4 * layer + at + n] = line.T
    swap.forward(1, 0, 1)
    shift_rows(fx, lanes, d0, rows, d0, ch, tc)
    finish(f_halo)
    own_sides(fl, fr, lanes, rows, d0, ch, tc)
    border_rows(fx, fl, fr, lanes, rows, d0, ch, tc)
    unroll = 4
    steps = rows // unroll
    turns = 4
    for turn in range(turns):

        @pl.loop(turn * steps // turns, (turn + 1) * steps // turns)
        def _(t):
            hidden = hidden_rows(lanes, w_first, t * unroll, unroll, d0, ch, tc, scale, 0)
            branch = jnp.dot(w_point[0], hidden, preferred_element_type=F32)
            for u in range(unroll):
                row = t * unroll + u
                y = branch[:, u * tc : (u + 1) * tc] * scale[1] + scale[3]
                y0[row] = (fx[d0 + row].astype(F32) + y).astype(BF16)

        swap.forward(0, turn, turns)

    def unpack(first, last):
        @pl.loop(first, last)
        def _(j):
            pieces = [mirror[h, j] for h in range(ratio)]
            for k in range(ratio):
                tx[d0 + ratio * j + k] = jnp.concatenate(
                    [x[:, k * rows : (k + 1) * rows] for x in pieces], axis=1
                )

    swap.arrive(1)
    unpack(swap.cut, half)
    start(t_halo[:1])
    swap.arrive(0)
    unpack(0, swap.cut)
    start(t_halo[1:2])
    pack_sides(tx, d0, tf, tlast, groups, tc)
    start(t_halo[2:])
    shift_rows(tx, lanes, d0, rows, d0, ch, tc)
    finish(t_halo)
    own_sides(tl, tr_, lanes, rows, d0, ch, tc)
    border_rows(tx, tl, tr_, lanes, rows, d0, ch, tc)

    def first_block(first, last):
        @pl.loop(first, last)
        def _(t):
            hidden = hidden_rows(lanes, w_turned, t * unroll, unroll, d0, ch, tc, scale, 0)
            branch = jnp.dot(w_point[0], hidden, preferred_element_type=F32)
            for u in range(unroll):
                row = t * unroll + u
                y = branch[:, u * tc : (u + 1) * tc] * scale[1] + scale[3]
                y = (tx[d0 + row].astype(F32) + y).astype(BF16).astype(F32)
                sx[d1 + row] = ((y + y0[row].astype(F32)) * 0.5).astype(BF16)

    edge = d1 // unroll
    first_block(0, edge)
    first_block(steps - edge, steps)
    start(s_halo[:2])
    first_block(edge, steps - edge)
    pack_sides(sx, d1, sf, slast, groups, tc)
    start(s_halo[2:])
    shift_rows(sx, lanes, d1, rows, d1, ch, tc)
    def second_block(first, last):
        @pl.loop(first, last)
        def _(t):
            hidden = hidden_rows(lanes, w_second, t * unroll, unroll, d1, ch, tc, scale, 1)
            branch = jnp.dot(w_point[1], hidden, preferred_element_type=F32)
            for u in range(unroll):
                row = t * unroll + u
                x = sx[d1 + row].astype(F32)
                both = []
                for v in (u, u + unroll):
                    y = branch[:, v * tc : (v + 1) * tc] * scale[5] + scale[7]
                    both.append((x + y).astype(BF16).astype(F32))
                out[row] = ((both[0] + both[1]) * 0.5).astype(BF16)

    finish(s_halo[2:4])
    own_sides(sl, sr, lanes, rows, d1, ch, tc)
    second_block(edge, steps - edge)
    finish(s_halo[:2] + s_halo[4:])
    border_rows(sx, sl, sr, lanes, rows, d1, ch, tc)
    second_block(0, edge)
    second_block(steps - edge, steps)

    swap.finish()
    finish_sends(f_halo)
    finish_sends(t_halo)
    finish_sends(s_halo)


def body(features, w_dilated, w_pointwise, norm_gain, norm_bias):
    n_row, n_col = lax.axis_size("row"), lax.axis_size("col")
    ch, rows, tc = features.shape
    ratio = tc // rows
    half = rows // ratio
    slots = ratio * (n_col // 2)
    tile = jnp.transpose(features, (1, 0, 2))
    turned = jnp.transpose(features, (2, 0, 1))
    w_taps = w_dilated.reshape(-1, ch, ch)
    d0, d1 = FIRST_DILATION, SECOND_DILATION
    groups = rows // PACK

    def vmem(*shape, dtype=BF16):
        return pltpu.VMEM(shape, dtype)

    def border(d):
        return vmem(groups + 2 * d // PACK, ch, tc)

    result = pl.pallas_call(
        functools.partial(kernel, n_row, n_col),
        out_shape=jax.ShapeDtypeStruct((rows, ch, tc), BF16),
        in_specs=[pl.BlockSpec(memory_space=pltpu.VMEM)] * 6,
        out_specs=pl.BlockSpec(memory_space=pltpu.VMEM),
        scratch_shapes=[
            vmem(rows + 2 * d0, ch, tc),
            vmem(rows + 2 * d0, ch, tc),
            vmem(rows + 2 * d1, ch, tc),
            border(d0), border(d0), border(d0), border(d0), border(d1), border(d1),
            *[vmem(groups, ch, tc) for _ in range(6)],
            vmem(rows, ch, tc),
            vmem(ratio, half, ch, tc),
            vmem(ratio, half, ch, tc),
            vmem(2, slots, half // 2, ch, tc),
            vmem(ch, 9 * ch),
            vmem(ch, 9 * ch),
            vmem(2 * ch, 9 * ch),
            vmem(rows + 2 * d1, 3 * ch, tc),
            vmem(8, ch, tc, dtype=F32),
            pltpu.SemaphoreType.DMA((3,)),
            pltpu.SemaphoreType.DMA((2, ratio)),
            pltpu.SemaphoreType.DMA((2, ratio)),
            pltpu.SemaphoreType.DMA((2, slots)),
            pltpu.SemaphoreType.DMA((2, slots)),
            pltpu.SemaphoreType.DMA((3, 8)),
            pltpu.SemaphoreType.DMA((3, 8)),
        ],
        compiler_params=pltpu.CompilerParams(
            collective_id=0, has_side_effects=True, vmem_limit_bytes=48 * 1024 * 1024
        ),
        cost_estimate=pl.CostEstimate(
            flops=4 * 2 * 9 * ch * ch * rows * tc, bytes_accessed=6 * ch * rows * tc, transcendentals=0
        ),
    )(tile, turned, w_taps, w_pointwise, norm_gain, norm_bias)
    return jnp.transpose(result, (1, 0, 2))


def solution(mesh):
    in_specs = (P(None, "row", "col"), P(), P(), P(), P())
    out_specs = P(None, "row", "col")
    return jax.shard_map(body, mesh=mesh, in_specs=in_specs, out_specs=out_specs, check_vma=False)
```

```python
import functools

import jax
import jax.numpy as jnp
from jax import lax
from jax.experimental import pallas as pl
from jax.experimental.pallas import tpu as pltpu
from jax.sharding import PartitionSpec as P

FIRST_DILATION = 8
SECOND_DILATION = 16
SIDE = 16
PACK = 8
MESH = pl.DeviceIdType.MESH
BF16 = jnp.bfloat16
F32 = jnp.float32

DIRECTIONS = ((1, 0), (-1, 0), (0, 1), (0, -1), (1, 1), (-1, 1), (1, -1), (-1, -1))


def inside(r, c, n_row, n_col):
    return (r >= 0) & (r < n_row) & (c >= 0) & (c < n_col)


def pack_sides(main, offset, side_first, side_last, first, last, tc):
    @pl.loop(first, last)
    def _(g):
        rows = [main[offset + g * PACK + k] for k in range(PACK)]
        side_first[g] = jnp.concatenate([x[:, :SIDE] for x in rows], axis=1)
        side_last[g] = jnp.concatenate([x[:, tc - SIDE :] for x in rows], axis=1)


def halo(main, left, right, side_first, side_last, d, tr, n_row, n_col, send, recv):
    r, c = lax.axis_index("row"), lax.axis_index("col")
    hg, groups = d // PACK, tr // PACK
    moves = []
    for n, (dr, dc) in enumerate(DIRECTIONS):
        if dc == 0:
            src = main.at[pl.ds(tr, d)] if dr == 1 else main.at[pl.ds(d, d)]
            dst = main.at[pl.ds(0, d)] if dr == 1 else main.at[pl.ds(tr + d, d)]
        else:
            from_ref = side_last if dc == 1 else side_first
            to_ref = left if dc == 1 else right
            if dr == 0:
                src, dst = from_ref, to_ref.at[pl.ds(hg, groups)]
            elif dr == 1:
                src, dst = from_ref.at[pl.ds(groups - hg, hg)], to_ref.at[pl.ds(0, hg)]
            else:
                src, dst = from_ref.at[pl.ds(0, hg)], to_ref.at[pl.ds(groups + hg, hg)]
        copy = pltpu.make_async_remote_copy(
            src_ref=src,
            dst_ref=dst,
            send_sem=send.at[n],
            recv_sem=recv.at[n],
            device_id=(r + dr, c + dc),
            device_id_type=MESH,
        )
        sends = inside(r + dr, c + dc, n_row, n_col)
        receives = inside(r - dr, c - dc, n_row, n_col)
        moves.append((copy, sends, receives, dst))
    return moves


def start(moves):
    for copy, sends, _, _ in moves:
        pl.when(sends)(copy.start)


def clear(moves):
    for _, _, receives, dst in moves:

        @pl.when(jnp.logical_not(receives))
        def _():
            dst[...] = jnp.zeros(dst.shape, dst.dtype)


def finish(moves):
    for copy, _, receives, _ in moves:
        pl.when(receives)(copy.wait_recv)


def finish_sends(moves):
    for copy, sends, _, _ in moves:
        pl.when(sends)(copy.wait_send)


def shift_rows(main, lanes, first, count, d, ch, tc):
    @pl.loop(0, count // PACK)
    def _(g):
        for k in range(PACK):
            e = first + g * PACK + k
            x = jnp.maximum(main[e], jnp.zeros((), BF16))
            lanes[e, :ch] = jnp.concatenate([x[:, tc - d :], x[:, : tc - d]], axis=1)
            lanes[e, ch : 2 * ch] = x
            lanes[e, 2 * ch :] = jnp.concatenate([x[:, d:], x[:, :d]], axis=1)


def patch_sides(left, right, lanes, first, last, d, ch, tc):
    @pl.loop(first, last)
    def _(g):
        lg = jnp.maximum(left[g], jnp.zeros((), BF16))
        rg = jnp.maximum(right[g], jnp.zeros((), BF16))
        for k in range(PACK):
            at = SIDE * k
            lanes[g * PACK + k, :ch, :d] = lg[:, at + SIDE - d : at + SIDE]
            lanes[g * PACK + k, 2 * ch :, tc - d :] = rg[:, at : at + d]


def border_rows(main, left, right, lanes, rows, d, ch, tc):
    shift_rows(main, lanes, 0, d, d, ch, tc)
    shift_rows(main, lanes, rows + d, d, d, ch, tc)
    hg, groups = d // PACK, rows // PACK
    patch_sides(left, right, lanes, 0, hg, d, ch, tc)
    patch_sides(left, right, lanes, hg + groups, 2 * hg + groups, d, ch, tc)


def own_sides(left, right, lanes, rows, d, ch, tc):
    first = d // PACK
    patch_sides(left, right, lanes, first, first + rows // PACK, d, ch, tc)


def hidden_rows(lanes, weights, row, count, d, ch, tc, scale, layer):
    columns = [
        jnp.concatenate([lanes[row + u + p * d] for p in range(3)], axis=0) for u in range(count)
    ]
    total = jnp.dot(
        weights[...], jnp.concatenate(columns, axis=1), preferred_element_type=F32
    )
    sets = []
    for base in range(0, weights.shape[0], ch):
        parts = [
            total[base : base + ch, u * tc : (u + 1) * tc] * scale[4 * layer]
            + scale[4 * layer + 2]
            for u in range(count)
        ]
        sets += [jnp.maximum(x, 0.0).astype(BF16) for x in parts]
    return jnp.concatenate(sets, axis=1)


def fill_weights(w_taps, w_first, w_turned, w_second, ch):
    for p in range(3):
        for q in range(3):
            at = (3 * p + q) * ch
            w_first[:, at : at + ch] = w_taps[3 * p + q]
            w_turned[:, at : at + ch] = w_taps[3 * q + p]
            w_second[:ch, at : at + ch] = w_taps[9 + 3 * p + q]
            w_second[ch:, at : at + ch] = w_taps[9 + 3 * q + p]


class Swap:
    def __init__(
        self, n_row, n_col, ratio, parcel, mirror, relay, local, m_send, m_recv, l_send, l_recv
    ):
        r, c = lax.axis_index("row"), lax.axis_index("col")
        self.me = (r, c)
        self.ratio = ratio
        self.local = local
        self.cut = parcel.shape[1] // 2
        mine = lax.rem(r, ratio)
        big = r // ratio
        odd, base = lax.rem(c, 2), c // 2
        slots = n_col // 2
        same = lambda a, b: (a[0] == b[0]) & (a[1] == b[1])
        part = lambda ref, piece: ref.at[pl.ds(piece * self.cut, self.cut)]

        def remote(src, dst, send, recv, to):
            return pltpu.make_async_remote_copy(
                src_ref=src, dst_ref=dst, send_sem=send, recv_sem=recv,
                device_id=to, device_id_type=MESH,
            )

        self.out = []
        for piece in (0, 1):
            for h in range(ratio):
                goal = (ratio * c + h, big)
                if piece == 0:
                    via = (ratio * c + mine, 2 * base + lax.rem(big, 2))
                    slot = (big // 2) * ratio + h
                else:
                    via = (ratio * big + h, 2 * (big // 2) + odd)
                    slot = base * ratio + mine
                stays = same(goal, self.me)
                short = same(via, goal) | same(via, self.me)
                src = part(parcel.at[h], piece)
                straight = remote(
                    src, part(mirror.at[mine], piece),
                    m_send.at[piece, h], m_recv.at[piece, mine], goal,
                )
                bent = remote(
                    src, relay.at[piece, slot],
                    m_send.at[piece, h], l_recv.at[piece, slot], via,
                )
                keep = pltpu.make_async_copy(
                    src, part(mirror.at[h], piece), local.at[1 + piece]
                )
                arrival = remote(
                    src, part(mirror.at[h], piece),
                    m_send.at[piece, h], m_recv.at[piece, h], goal,
                )
                no = jnp.logical_not
                self.out.append(
                    dict(
                        goal=goal, via=via, piece=piece, h=h, stays=stays,
                        straight=no(stays) & short, bent=no(stays) & no(short),
                        straight_copy=straight, bent_copy=bent, keep=keep, arrival=arrival,
                    )
                )

        self.through = []
        relays = (big // 2) == base
        for piece in (0, 1):
            for m in range(slots):
                for k in range(ratio):
                    if piece == 0:
                        source = (ratio * (2 * m + odd) + mine, big)
                        goal = (ratio * big + k, 2 * m + odd)
                        h = k
                    else:
                        source = (ratio * big + k, 2 * m + odd)
                        goal = (ratio * (2 * m + odd) + mine, big)
                        h = mine
                    theirs = lax.rem(source[0], ratio)
                    slot = m * ratio + k
                    when = (
                        relays
                        & jnp.logical_not(same(source, self.me))
                        & jnp.logical_not(same(goal, self.me))
                        & jnp.logical_not(same(goal, source))
                    )
                    copy = remote(
                        relay.at[piece, slot], part(mirror.at[theirs], piece),
                        l_send.at[piece, slot], m_recv.at[piece, theirs], goal,
                    )
                    arrival = remote(
                        relay.at[piece, slot], relay.at[piece, slot],
                        l_send.at[piece, slot], l_recv.at[piece, slot], source,
                    )
                    self.through.append((piece, when, source, copy, arrival))

        self.into = []
        for piece in (0, 1):
            for h in range(ratio):
                source = (ratio * c + h, big)
                sb, so = source[0] // ratio, lax.rem(source[0], ratio)
                if piece == 0:
                    via = (ratio * big + so, 2 * (big // 2) + lax.rem(sb, 2))
                else:
                    via = (ratio * sb + mine, 2 * (sb // 2) + lax.rem(big, 2))
                stays = same(source, self.me)
                short = same(via, source) | same(via, self.me)
                self.into.append((source, via, stays, short))

    def greet(self, barrier, expected):
        def signal(when, to):
            @pl.when(when)
            def _():
                pl.semaphore_signal(barrier, inc=1, device_id=to, device_id_type=MESH)

        for source, via, stays, short in self.into:
            no = jnp.logical_not
            signal(no(stays) & short, source)
            signal(no(stays) & no(short), via)
        for _, when, source, _, _ in self.through:
            signal(when, source)
            expected = expected + when.astype(jnp.int32)
        for x in self.out:
            expected = expected + jnp.logical_not(x["stays"]).astype(jnp.int32)
        return expected

    def start(self):
        for x in self.out:
            pl.when(x["bent"])(x["bent_copy"].start)
        for x in self.out:
            pl.when(x["straight"])(x["straight_copy"].start)
            pl.when(x["stays"])(x["keep"].start)

    def forward(self, piece, turn, turns):
        passing = [x for x in self.through if x[0] == piece]
        share = -(-len(passing) // turns)
        for _, when, _, copy, arrival in passing[turn * share : (turn + 1) * share]:

            @pl.when(when)
            def _():
                arrival.wait_recv()
                copy.start()

    def arrive(self, piece):
        for x in self.out[piece * self.ratio : (piece + 1) * self.ratio]:
            pl.when(jnp.logical_not(x["stays"]))(x["arrival"].wait_recv)
            pl.when(x["stays"])(x["keep"].wait)

    def finish(self):
        for x in self.out:
            pl.when(jnp.logical_not(x["stays"]))(x["straight_copy"].wait_send)
        for _, when, _, copy, _ in self.through:
            pl.when(when)(copy.wait_send)


def kernel(
    n_row, n_col, tile, turned, w_taps, w_point, gain, bias, out,
    fx, tx, sx, fl, fr, tl, tr_, sl, sr, ff, flast, tf, tlast, sf, slast,
    y0, parcel, mirror, relay, w_first, w_turned, w_second, lanes, scale,
    local, m_send, m_recv, l_send, l_recv, h_send, h_recv,
):
    r, c = lax.axis_index("row"), lax.axis_index("col")
    rows, ch, tc = tile.shape
    ratio = tc // rows
    d0, d1 = FIRST_DILATION, SECOND_DILATION

    own = pltpu.make_async_copy(tile, fx.at[pl.ds(d0, rows)], local.at[0])
    own.start()

    swap = Swap(n_row, n_col, ratio, parcel, mirror, relay, local, m_send, m_recv, l_send, l_recv)

    barrier = pltpu.get_barrier_semaphore()
    expected = jnp.int32(0)
    for dr, dc in DIRECTIONS:
        there = inside(r + dr, c + dc, n_row, n_col)
        expected = expected + there.astype(jnp.int32)

        @pl.when(there)
        def _():
            pl.semaphore_signal(
                barrier, inc=1, device_id=(r + dr, c + dc), device_id_type=MESH
            )

    expected = swap.greet(barrier, expected)

    half = rows // ratio
    groups = rows // PACK

    @pl.loop(0, half)
    def _(j):
        for h in range(ratio):
            pair = [turned[h * rows + ratio * j + k] for k in range(ratio)]
            parcel[h, j] = jnp.concatenate(pair, axis=1)

    own.wait()
    pack_sides(fx, d0, ff, flast, 0, groups, tc)
    f_halo = halo(fx, fl, fr, ff, flast, d0, rows, n_row, n_col, h_send.at[0], h_recv.at[0])
    pl.semaphore_wait(barrier, expected)

    start(f_halo)
    swap.start()

    t_halo = halo(tx, tl, tr_, tf, tlast, d0, rows, n_row, n_col, h_send.at[1], h_recv.at[1])
    s_halo = halo(sx, sl, sr, sf, slast, d1, rows, n_row, n_col, h_send.at[2], h_recv.at[2])
    clear(f_halo)
    clear(t_halo)
    clear(s_halo)
    fill_weights(w_taps, w_first, w_turned, w_second, ch)
    for layer in range(2):
        for n in range(2):
            for at, ref in ((0, gain), (2, bias)):
                line = jnp.broadcast_to(ref[layer, n : n + 1, :], (tc, ch))
                scale[4 * layer + at + n] = line.T
    swap.forward(1, 0, 1)
    shift_rows(fx, lanes, d0, rows, d0, ch, tc)
    finish(f_halo)
    own_sides(fl, fr, lanes, rows, d0, ch, tc)
    border_rows(fx, fl, fr, lanes, rows, d0, ch, tc)
    unroll = 4
    steps = rows // unroll
    turns = 4
    for turn in range(turns):

        @pl.loop(turn * steps // turns, (turn + 1) * steps // turns)
        def _(t):
            hidden = hidden_rows(lanes, w_first, t * unroll, unroll, d0, ch, tc, scale, 0)
            branch = jnp.dot(w_point[0], hidden, preferred_element_type=F32)
            for u in range(unroll):
                row = t * unroll + u
                y = branch[:, u * tc : (u + 1) * tc] * scale[1] + scale[3]
                y0[row] = (fx[d0 + row].astype(F32) + y).astype(BF16)

        swap.forward(0, turn, turns)

    def unpack(first, last):
        @pl.loop(first, last)
        def _(j):
            pieces = [mirror[h, j] for h in range(ratio)]
            for k in range(ratio):
                tx[d0 + ratio * j + k] = jnp.concatenate(
                    [x[:, k * rows : (k + 1) * rows] for x in pieces], axis=1
                )

    def first_block(first, last):
        @pl.loop(first, last)
        def _(t):
            hidden = hidden_rows(lanes, w_turned, t * unroll, unroll, d0, ch, tc, scale, 0)
            branch = jnp.dot(w_point[0], hidden, preferred_element_type=F32)
            for u in range(unroll):
                row = t * unroll + u
                y = branch[:, u * tc : (u + 1) * tc] * scale[1] + scale[3]
                y = (tx[d0 + row].astype(F32) + y).astype(BF16).astype(F32)
                sx[d1 + row] = ((y + y0[row].astype(F32)) * 0.5).astype(BF16)

    swap.arrive(1)
    unpack(swap.cut, half)
    start(t_halo[:1])
    upper = groups // 2
    pack_sides(tx, d0, tf, tlast, upper, groups, tc)
    shift_rows(tx, lanes, d0 + upper * PACK, rows - upper * PACK, d0, ch, tc)
    swap.arrive(0)
    unpack(0, swap.cut)
    start(t_halo[1:2])
    pack_sides(tx, d0, tf, tlast, 0, upper, tc)
    start(t_halo[2:])
    shift_rows(tx, lanes, d0, upper * PACK, d0, ch, tc)
    finish(t_halo[2:4])
    own_sides(tl, tr_, lanes, rows, d0, ch, tc)
    inner, edge = d0 // unroll, d1 // unroll
    first_block(inner, edge)
    first_block(steps - edge, steps - inner)
    finish(t_halo[:2] + t_halo[4:])
    border_rows(tx, tl, tr_, lanes, rows, d0, ch, tc)

    first_block(0, inner)
    first_block(steps - inner, steps)
    start(s_halo[:2])
    first_block(edge, steps - edge)
    pack_sides(sx, d1, sf, slast, 0, groups, tc)
    start(s_halo[2:])
    shift_rows(sx, lanes, d1, rows, d1, ch, tc)
    def second_block(first, last):
        @pl.loop(first, last)
        def _(t):
            hidden = hidden_rows(lanes, w_second, t * unroll, unroll, d1, ch, tc, scale, 1)
            branch = jnp.dot(w_point[1], hidden, preferred_element_type=F32)
            for u in range(unroll):
                row = t * unroll + u
                x = sx[d1 + row].astype(F32)
                both = []
                for v in (u, u + unroll):
                    y = branch[:, v * tc : (v + 1) * tc] * scale[5] + scale[7]
                    both.append((x + y).astype(BF16).astype(F32))
                out[row] = ((both[0] + both[1]) * 0.5).astype(BF16)

    finish(s_halo[2:4])
    own_sides(sl, sr, lanes, rows, d1, ch, tc)
    second_block(edge, steps - edge)
    finish(s_halo[:2] + s_halo[4:])
    border_rows(sx, sl, sr, lanes, rows, d1, ch, tc)
    second_block(0, edge)
    second_block(steps - edge, steps)

    swap.finish()
    finish_sends(f_halo)
    finish_sends(t_halo)
    finish_sends(s_halo)


def body(features, w_dilated, w_pointwise, norm_gain, norm_bias):
    n_row, n_col = lax.axis_size("row"), lax.axis_size("col")
    ch, rows, tc = features.shape
    ratio = tc // rows
    half = rows // ratio
    slots = ratio * (n_col // 2)
    tile = jnp.transpose(features, (1, 0, 2))
    turned = jnp.transpose(features, (2, 0, 1))
    w_taps = w_dilated.reshape(-1, ch, ch)
    d0, d1 = FIRST_DILATION, SECOND_DILATION
    groups = rows // PACK

    def vmem(*shape, dtype=BF16):
        return pltpu.VMEM(shape, dtype)

    def border(d):
        return vmem(groups + 2 * d // PACK, ch, tc)

    result = pl.pallas_call(
        functools.partial(kernel, n_row, n_col),
        out_shape=jax.ShapeDtypeStruct((rows, ch, tc), BF16),
        in_specs=[pl.BlockSpec(memory_space=pltpu.VMEM)] * 6,
        out_specs=pl.BlockSpec(memory_space=pltpu.VMEM),
        scratch_shapes=[
            vmem(rows + 2 * d0, ch, tc),
            vmem(rows + 2 * d0, ch, tc),
            vmem(rows + 2 * d1, ch, tc),
            border(d0), border(d0), border(d0), border(d0), border(d1), border(d1),
            *[vmem(groups, ch, tc) for _ in range(6)],
            vmem(rows, ch, tc),
            vmem(ratio, half, ch, tc),
            vmem(ratio, half, ch, tc),
            vmem(2, slots, half // 2, ch, tc),
            vmem(ch, 9 * ch),
            vmem(ch, 9 * ch),
            vmem(2 * ch, 9 * ch),
            vmem(rows + 2 * d1, 3 * ch, tc),
            vmem(8, ch, tc, dtype=F32),
            pltpu.SemaphoreType.DMA((3,)),
            pltpu.SemaphoreType.DMA((2, ratio)),
            pltpu.SemaphoreType.DMA((2, ratio)),
            pltpu.SemaphoreType.DMA((2, slots)),
            pltpu.SemaphoreType.DMA((2, slots)),
            pltpu.SemaphoreType.DMA((3, 8)),
            pltpu.SemaphoreType.DMA((3, 8)),
        ],
        compiler_params=pltpu.CompilerParams(
            collective_id=0, has_side_effects=True, vmem_limit_bytes=48 * 1024 * 1024
        ),
        cost_estimate=pl.CostEstimate(
            flops=4 * 2 * 9 * ch * ch * rows * tc, bytes_accessed=6 * ch * rows * tc, transcendentals=0
        ),
    )(tile, turned, w_taps, w_pointwise, norm_gain, norm_bias)
    return jnp.transpose(result, (1, 0, 2))


def solution(mesh):
    in_specs = (P(None, "row", "col"), P(), P(), P(), P())
    out_specs = P(None, "row", "col")
    return jax.shard_map(body, mesh=mesh, in_specs=in_specs, out_specs=out_specs, check_vma=False)
```
